512 devices in a mesh: expert: 64 (over z, y_hi, core), tensor: 8 (over x, y_lo).
Axes of the slice: x: 4, y: 8 (y_hi: 4, y_lo: 2; y = y_hi * 2 + y_lo), z: 8, core: 2. Of those that a mesh axis runs over, the one named last changes fastest.
Arguments:
- out_grad: bfloat16 [8192, 3584], P('expert', 'tensor'), may hold values from -6 to 6
- gate_probs: float32 [8192, 2], P('expert'), may hold values from 0.2 to 1
- expert_ids: int32 [8192, 2], P('expert'), may hold values from 0 to 31, all different within a row; in each aligned block of 128 rows (0 to 127, 128 to 255, ...) at most 10 rows name the same one
- saved_gate: bfloat16 [77824, 640], P(('expert', 'tensor')), may hold values from -6 to 6
- saved_up: bfloat16 [77824, 640], P(('expert', 'tensor')), may hold values from -6 to 6
- w_gate: bfloat16 [77824, 3584], P(('expert', 'tensor')), may hold values from -0.078125 to 0.078125
- w_up: bfloat16 [77824, 3584], P(('expert', 'tensor')), may hold values from -0.078125 to 0.078125
- w_down: bfloat16 [77824, 3584], P(('expert', 'tensor')), may hold values from -0.09375 to 0.09375
Outputs:
- in_grad: bfloat16 [8192, 3584], P('expert', 'tensor')
The draws below stay inside these ranges and needn't reach their ends.
Inputs may be any that keep to these rules, and one draw needn't show every extreme that they name: `expert_ids`: each row names 2 different experts. Among the 128 rows of one device no expert is named more than 10 times, a bound that some block reaches there in some device.
All inputs are finite; a program needn't handle non-finite values.
Results may differ from the reference program's by a relative error of at most 0.017.
Values may be sent and summed in bfloat16 or wider, within the bound.
No kernel may reach another device: no remote copies, remote signals or barrier semaphores. Data moves between devices by JAX's collectives and lax.ppermute only.
A program may use at most 128 MiB of HBM per device.

```python
import math
import jax
import jax.numpy as jnp
import numpy as np
from jax import lax

D = 3584
FF = 2432
TOPK = 2
TOK_DEV = 128
EXPERTS = 32
CAP = 10
TOKENS = 8192
N_EXPERT = 64
N_TENSOR = 8


def levels(own_key, shape, shards, least, top_value):
    gain = 1.0
    for position, blocks in shards:
        steps = jax.random.uniform(jax.random.fold_in(jax.random.fold_in(own_key, 6), position), (blocks,), jnp.float32, least / len(shards), top_value / len(shards))
        gain = gain * jnp.repeat(jnp.exp(steps), shape[position] // blocks).reshape((-1,) + (1,) * (len(shape) - 1 - position))
    return gain


def assign_block(rng, own, number, rows, number_of, top, most, lean):
    order = jax.random.permutation(rng, number_of)
    heavy_load, common = load_shares(number_of, rows * top, most, lean, True), load_shares(number_of, rows * top, most, lean, False)
    places = jnp.arange(number_of)

    def named(sizes, turn):
        used = int((sizes > 0).sum())
        fixed = max(1, used // 4)
        moved = fixed + (places - fixed + turn * (used - fixed)) % max(1, number_of - fixed)
        return jnp.zeros((number_of,), jnp.int32).at[order[jnp.where(places < fixed, places, moved)]].set(jnp.asarray(sizes, jnp.int32))

    sizes = jnp.where(number % 4 == 0, named(heavy_load, number // 4), named(common, number - number // 4 - 1))
    mixed = jax.random.permutation(jax.random.fold_in(own, 3), number_of)
    donor, receiver = mixed[0:number_of // 2 * 2:2], mixed[1:number_of // 2 * 2:2]
    slack = jnp.minimum(sizes[donor] - 1, most - sizes[receiver]) // 2
    slack = jnp.where((donor == order[0]) | (receiver == order[0]) | (sizes[receiver] == 0), 0, jnp.maximum(slack, 0))
    moved = jax.random.randint(jax.random.fold_in(own, 4), (number_of // 2,), 0, 1 << 20) % (slack + 1)
    sizes = sizes.at[donor].add(-moved).at[receiver].add(moved)
    items = jnp.searchsorted(jnp.cumsum(sizes), jnp.arange(rows * top), side="right").astype(jnp.int32)
    listing = items.reshape(top, rows).T
    listing = listing[jax.random.permutation(jax.random.fold_in(own, 1), rows)]
    turn = jax.random.randint(jax.random.fold_in(own, 2), (rows, 1), 0, top)
    return jnp.take_along_axis(listing, (jnp.arange(top)[None, :] + turn) % top, axis=1)


def load_shares(amount, total, most, lean, full):
    loads = [(1 << 20) // math.isqrt(grade ** lean) + 1 for grade in range(1, amount + 1)]
    largest = most if full else min(most, max(-(-total // amount), total * loads[0] // sum(loads)))
    least = 1 if total - largest >= amount - 1 else 0
    counts, spare = [largest] + [least] * (amount - 1), total - largest - least * (amount - 1)
    while spare > 0:
        movable = [i for i in range(1, amount) if counts[i] < largest] or [i for i in range(1, amount) if counts[i] < most]
        mass, budget = sum([loads[i] for i in movable]), spare
        for i in movable:
            addition = min(most - counts[i], max(1, budget * loads[i] // mass), spare)
            counts[i] = counts[i] + addition
            spare = spare - addition
    return np.array(counts)


def gaussian(key, dims, width, limit, shards=(), kind=jnp.bfloat16):
    gain = levels(key, dims, shards, -0.22, 0.18) if shards else 1.0
    drawn = jax.random.normal(key, dims, jnp.float32) * width * gain
    return jnp.minimum(jnp.maximum(drawn, -limit), limit).astype(kind)


def setup_inputs(seed: int = 0) -> dict:
    splits = jax.random.split(jax.random.key(seed), 9)
    out_grad = gaussian(splits[0], (TOKENS, D), 1.0, 6.0, ((0, 64), (1, 8)))
    gate_probs = jnp.clip(0.2 + 0.8 * jax.random.uniform(splits[1], (TOKENS, TOPK), jnp.float32) ** levels(splits[1], (TOKENS, TOPK), ((0, 64),), -0.2, 0.2), 0.2, 1.0)
    expert_ids_keys = jax.random.split(jax.random.fold_in(splits[2], 1), TOKENS // TOK_DEV)
    expert_ids_turns = jax.random.permutation(jax.random.fold_in(splits[2], 3), TOKENS // TOK_DEV)
    expert_ids = jax.vmap(lambda own, number: assign_block(jax.random.fold_in(splits[2], 2), own, number, TOK_DEV, EXPERTS, TOPK, CAP, 1))(expert_ids_keys, expert_ids_turns).reshape((TOKENS, TOPK))
    saved_gate = gaussian(splits[3], (EXPERTS * FF, N_EXPERT * CAP), 1.0, 6.0, ((0, 512),))
    saved_up = gaussian(splits[4], (EXPERTS * FF, N_EXPERT * CAP), 1.0, 6.0, ((0, 512),))
    w_gate = gaussian(splits[5], (EXPERTS * FF, D), (2 * FF) ** -0.5, 0.078125, ((0, 512),))
    w_up = gaussian(splits[6], (EXPERTS * FF, D), (2 * FF) ** -0.5, 0.078125, ((0, 512),))
    w_down = gaussian(splits[7], (EXPERTS * FF, D), D ** -0.5, 0.09375, ((0, 512),))
    return {"out_grad": out_grad, "gate_probs": gate_probs, "expert_ids": expert_ids, "saved_gate": saved_gate, "saved_up": saved_up, "w_gate": w_gate, "w_up": w_up, "w_down": w_down}


def reference(out_grad, gate_probs, expert_ids, saved_gate, saved_up, w_gate, w_up, w_down):
    blocks = expert_ids.reshape(N_EXPERT, TOK_DEV * TOPK)
    onehot = (blocks[:, :, None] == jnp.arange(EXPERTS, dtype=jnp.int32)[None, None, :]).astype(jnp.int32)
    before = jnp.cumsum(onehot, axis=1) - onehot
    slot_index = jnp.sum(before * onehot, axis=2).astype(jnp.int32)
    source = jnp.arange(N_EXPERT, dtype=jnp.int32)[:, None]
    destination = (blocks * (N_EXPERT * CAP) + source * CAP + slot_index).reshape(-1).astype(jnp.int32)
    scaled = (gate_probs[:, :, None] * out_grad[:, None, :].astype(jnp.float32)).astype(jnp.bfloat16)
    scaled = scaled.reshape(TOKENS * TOPK, D)
    routed = jnp.zeros((EXPERTS * N_EXPERT * CAP, D), jnp.bfloat16).at[destination].set(scaled)
    routed = routed.reshape(EXPERTS, N_EXPERT * CAP, D)
    groups = 2 * N_TENSOR
    group_width = FF // groups
    slot_rows = N_EXPERT * CAP

    def one_expert(expert):
        routed_rows = routed[expert]
        first = (expert * FF).astype(jnp.int32)
        gate_rows = lax.dynamic_slice_in_dim(w_gate, first, FF, 0)
        up_rows = lax.dynamic_slice_in_dim(w_up, first, FF, 0)
        down_rows = lax.dynamic_slice_in_dim(w_down, first, FF, 0)
        gate_vals = lax.dynamic_slice_in_dim(saved_gate, first, FF, 0).astype(jnp.float32).T
        up_vals = lax.dynamic_slice_in_dim(saved_up, first, FF, 0).astype(jnp.float32).T
        hidden_grad = jnp.dot(routed_rows, down_rows.T, preferred_element_type=jnp.float32)
        logistic = jax.nn.sigmoid(gate_vals)
        grad_gate = (hidden_grad * up_vals * logistic * (1.0 + gate_vals * (1.0 - logistic))).astype(jnp.bfloat16)
        grad_up = (hidden_grad * gate_vals * logistic).astype(jnp.bfloat16)
        gate_part = grad_gate.astype(jnp.float32).reshape(slot_rows, groups, group_width)
        up_part = grad_up.astype(jnp.float32).reshape(slot_rows, groups, group_width)
        gate_mat = gate_rows.astype(jnp.float32).reshape(groups, group_width, D)
        up_mat = up_rows.astype(jnp.float32).reshape(groups, group_width, D)
        part = jnp.einsum('sjw,jwd->jsd', gate_part, gate_mat) + jnp.einsum('sjw,jwd->jsd', up_part, up_mat)
        part = lax.optimization_barrier(part.astype(jnp.bfloat16)).astype(jnp.float32)
        return jnp.sum(part, axis=0)

    totals = lax.map(one_expert, jnp.arange(EXPERTS, dtype=jnp.int32))
    flattened = totals.reshape(EXPERTS * slot_rows, D)
    picked = jnp.take(flattened, destination, axis=0).reshape(TOKENS, TOPK, D)
    return jnp.sum(picked, axis=1).astype(jnp.bfloat16)
```

```python
import jax
import jax.numpy as jnp
from jax import lax
from jax.experimental import pallas as pl
from jax.experimental.pallas import tpu as pltpu
from jax.sharding import Mesh, PartitionSpec as P

CAP = 10
HALF = CAP // 2
BLK = 40
EXP = 32
TEN = 8
TOK = 128
FEAT = 448
FULL = 384
FF = 152
D = 3584
PAIR = 2 * FEAT
ROWS = EXP * CAP
HROWS = ROWS // 2
PIECE = 7 * HROWS
GRP = EXP // 2

BF = jnp.bfloat16
F32 = jnp.float32
VM = pl.BlockSpec(memory_space=pltpu.VMEM)
SM = pl.BlockSpec(memory_space=pltpu.SMEM)


def nt(a, b):
    return lax.dot_general(a, b, (((1,), (1,)), ((), ())), preferred_element_type=F32)


def tn(a, b):
    return lax.dot_general(a, b, (((0,), (0,)), ((), ())), preferred_element_type=F32)


def block_ids():
    e = lax.broadcasted_iota(jnp.int32, (EXP, BLK, TOK), 0).reshape(EXP * BLK, TOK)
    k = lax.broadcasted_iota(jnp.int32, (EXP, BLK, TOK), 1).reshape(EXP * BLK, TOK)
    return e, k


def slots_of(e, k):
    tens = jnp.where(k >= 30, 30, jnp.where(k >= 20, 20, jnp.where(k >= 10, 10, 0)))
    low = jnp.where(k < 35, e * CAP + k - tens, -1)
    high = jnp.where((k >= 30) & (k < 35), e * CAP + k - 30 + HALF, -1)
    return low, high


def pack_kernel(pos_ref, xt_ref, gt_ref, et_ref, out_ref, tgt_ref):
    yl = pos_ref[1]
    e0 = et_ref[0:1, :]
    e1 = et_ref[1:2, :]
    xi = lax.broadcasted_iota(jnp.int32, (EXP, TOK), 0)
    named = ((xi == e0) | (xi == e1)).astype(F32).astype(BF)
    earlier = (
        lax.broadcasted_iota(jnp.int32, (TOK, TOK), 0) < lax.broadcasted_iota(jnp.int32, (TOK, TOK), 1)
    ).astype(F32).astype(BF)
    before = jnp.dot(named, earlier, preferred_element_type=F32)
    s0 = jnp.sum(jnp.where(xi == e0, before, 0.0), axis=0, keepdims=True).astype(jnp.int32)
    s1 = jnp.sum(jnp.where(xi == e1, before, 0.0), axis=0, keepdims=True).astype(jnp.int32)
    t0 = e0 * CAP + s0
    t1 = e1 * CAP + s1
    tgt_ref[0:1, :] = t0
    tgt_ref[1:2, :] = t1
    e, k = block_ids()
    low, high = slots_of(e, k)
    one = lambda hit: hit.astype(F32).astype(BF)
    m_low = jnp.concatenate([one(low == t0), one(low == t1)], axis=1)
    m_high = jnp.concatenate([one(high == t0), one(high == t1)], axis=1)

    def scaled(rows):
        x = rows.astype(F32)
        return jnp.concatenate([(x * gt_ref[0:1, :]).astype(BF), (x * gt_ref[1:2, :]).astype(BF)], axis=1)

    full = scaled(xt_ref[pl.ds(pl.multiple_of(64 * yl, 64), FULL), :])
    half = scaled(xt_ref[pl.ds(pl.multiple_of(FULL * (1 - yl), 64), 64), :])
    none = jnp.zeros_like(half)
    wide = nt(m_low, full)
    pair = nt(m_low, jnp.concatenate([half, none], axis=0)) + nt(m_high, jnp.concatenate([none, half], axis=0))
    picked = jnp.where(
        k < 10, wide[:, 0:128], jnp.where(k < 20, wide[:, 128:256], jnp.where(k < 30, wide[:, 256:384], pair))
    )
    out_ref[...] = picked.astype(BF)


def sort_kernel(in_ref, out_ref):
    n_out, n_in = 7 * GRP * HALF, GRP * BLK
    rows = GRP * HALF
    q = lax.broadcasted_iota(jnp.int32, (rows, n_in), 0)
    col = lax.broadcasted_iota(jnp.int32, (rows, n_in), 1)
    gap = col - 35 * ((q * 205) >> 10) - q
    moves = jnp.concatenate([(gap == HALF * b).astype(F32).astype(BF) for b in range(7)], axis=0)
    both = jnp.concatenate([in_ref[0:n_in, :], in_ref[n_in : 2 * n_in, :]], axis=1)
    res = jnp.dot(moves, both, preferred_element_type=F32).astype(BF)
    for b in range(7):
        for g in range(2):
            block = res[b * rows : (b + 1) * rows, g * 128 : (g + 1) * 128]
            for t in range(TEN):
                at = t * PIECE + b * HROWS + g * rows
                out_ref[at : at + rows, :] = block


def main_kernel(pos_ref, in_ref, wd0, wd1, wg0, wg1, wu0, wu1, sg0, sg1, su0, su1, out_ref, r_ref):
    core = pos_ref[2]
    for i in range(4):
        base, even, odd = i * PAIR, 2 * i * PIECE, (2 * i + 1) * PIECE
        for j in range(3):
            r_ref[:, base + 128 * j : base + 128 * (j + 1)] = in_ref[even + j * ROWS : even + (j + 1) * ROWS, :]
            at = base + 512 + 128 * j
            r_ref[:, at : at + 128] = in_ref[odd + j * ROWS : odd + (j + 1) * ROWS, :]
        eh = in_ref[even + 3 * ROWS : even + PIECE, :]
        oh = in_ref[odd + 3 * ROWS : odd + PIECE, :]
        r_ref[0:HROWS, base + FULL : base + 512] = jnp.concatenate([eh[:, :64], oh[:, :64]], axis=1)
        r_ref[HROWS:ROWS, base + FULL : base + 512] = jnp.concatenate([eh[:, 64:], oh[:, 64:]], axis=1)

    n_col = 2 * ROWS
    row = lax.broadcasted_iota(jnp.int32, (n_col, ROWS), 0)
    r = lax.broadcasted_iota(jnp.int32, (n_col, ROWS), 1)
    h = (r >= HROWS).astype(jnp.int32)
    q = r - HROWS * h
    pick = (row == 15 * ((q * 205) >> 10) + q + HALF * h + CAP * core).astype(F32).astype(BF)

    grads = []
    for wd, sg, su, wg, wu in ((wd0, sg0, su0, wg0, wu0), (wd1, sg1, su1, wg1, wu1)):
        hidden = nt(wd[...], r_ref[...])
        g = jnp.dot(sg[...], pick, preferred_element_type=F32)
        u = jnp.dot(su[...], pick, preferred_element_type=F32)
        sig = 1.0 / (1.0 + jnp.exp(-g))
        gate = hidden * u * sig * (1.0 + g * (1.0 - sig))
        up = hidden * g * sig
        grads.append((gate.T.astype(BF), wg))
        grads.append((up.T.astype(BF), wu))

    for i in range(4):
        base, even, odd = i * PAIR, 2 * i * PIECE, (2 * i + 1) * PIECE
        acc = None
        for grad, w in grads:
            term = jnp.dot(grad, w[:, base : base + PAIR], preferred_element_type=F32)
            acc = term if acc is None else acc + term
        acc = acc.astype(BF)
        for j in range(3):
            out_ref[even + j * ROWS : even + (j + 1) * ROWS, :] = acc[:, 128 * j : 128 * (j + 1)]
            out_ref[odd + j * ROWS : odd + (j + 1) * ROWS, :] = acc[:, 512 + 128 * j : 512 + 128 * (j + 1)]
        lo = acc[0:HROWS, FULL:512]
        hi = acc[HROWS:ROWS, FULL:512]
        out_ref[even + 3 * ROWS : even + PIECE, :] = jnp.concatenate([lo[:, :64], hi[:, :64]], axis=1)
        out_ref[odd + 3 * ROWS : odd + PIECE, :] = jnp.concatenate([lo[:, 64:], hi[:, 64:]], axis=1)


def unsort_kernel(in_ref, out_ref):
    rows = GRP * HALF
    n_out = GRP * BLK
    q = lax.broadcasted_iota(jnp.int32, (n_out, rows), 1)
    row = lax.broadcasted_iota(jnp.int32, (n_out, rows), 0)
    gap = row - 35 * ((q * 205) >> 10) - q
    res = [None, None]
    for b in range(7):
        move = (gap == HALF * b).astype(F32).astype(BF)
        cols = []
        for g in range(2):
            total = None
            for t in range(TEN):
                at = t * PIECE + b * HROWS + g * rows
                part = in_ref[at : at + rows, :].astype(F32)
                total = part if total is None else total + part
            cols.append(total.astype(BF))
        term = jnp.dot(move, jnp.concatenate(cols, axis=1), preferred_element_type=F32)
        for g in range(2):
            t = term[:, g * 128 : (g + 1) * 128]
            res[g] = t if res[g] is None else res[g] + t
    for g in range(2):
        out_ref[g * n_out : (g + 1) * n_out, :] = res[g].astype(BF)


def combine_kernel(pos_ref, in_ref, tgt_ref, out_ref):
    yl = pos_ref[1]
    t0 = tgt_ref[0:1, :]
    t1 = tgt_ref[1:2, :]
    e, k = block_ids()
    low, high = slots_of(e, k)
    hit = ((low == t0) | (low == t1)).astype(F32)
    cut = lambda a, b: jnp.where((k >= a) & (k < b), hit, 0.0).astype(BF)
    hit_high = ((high == t0) | (high == t1)).astype(F32).astype(BF)
    take = jnp.concatenate([cut(0, 10), cut(10, 20), cut(20, 30), cut(30, 35), hit_high], axis=1)
    res = tn(in_ref[...], take)
    start = pl.multiple_of(64 * yl, 64)
    for j in range(3):
        out_ref[pl.ds(pl.multiple_of(start + 128 * j, 64), 128), :] = res[:, 128 * j : 128 * (j + 1)].astype(BF)
    half = res[0:64, FULL:512] + res[64:128, 512:640]
    out_ref[pl.ds(pl.multiple_of(FULL * (1 - yl), 64), 64), :] = half.astype(BF)


def call(kernel, outs, specs, flops=0, moved=0, scratch=(), limit=16):
    many = isinstance(outs, (list, tuple))
    return pl.pallas_call(
        kernel,
        out_shape=outs,
        in_specs=specs,
        out_specs=[VM] * len(outs) if many else VM,
        scratch_shapes=list(scratch),
        cost_estimate=pl.CostEstimate(flops=flops, bytes_accessed=moved, transcendentals=0),
        compiler_params=pltpu.CompilerParams(vmem_limit_bytes=limit << 20),
    )


def sds(shape, dtype=BF):
    return jax.ShapeDtypeStruct(shape, dtype)


def swap_core(a):
    return lax.ppermute(a, "core", [(0, 1), (1, 0)])


def exchange(a, axes, n):
    blocks = a.reshape(n, a.shape[0] // n, a.shape[1])
    return lax.all_to_all(blocks, axes, split_axis=0, concat_axis=0, tiled=True).reshape(a.shape)


def shards(out_grad, gate_probs, expert_ids, saved_gate, saved_up, w_gate, w_up, w_down):
    pos = jnp.stack([lax.axis_index("x"), lax.axis_index("yl"), lax.axis_index("core")]).astype(jnp.int32)
    packed, target = call(
        pack_kernel, [sds((EXP * BLK, 128)), sds((2, TOK), jnp.int32)], [SM, VM, VM, VM], 10**9, 10**6
    )(pos, out_grad.T, gate_probs.T, expert_ids.T)
    got = exchange(packed, ("z", "yh"), EXP)
    spread = call(sort_kernel, sds((TEN * PIECE, 128)), [VM], 10**9, 10**6)(got)
    pieces = exchange(spread, ("x", "yl"), TEN)
    operands = []
    for a in (w_down, w_gate, w_up, saved_gate, saved_up):
        operands += [a, swap_core(a)]
    parts = call(
        main_kernel,
        sds((TEN * PIECE, 128)),
        [SM] + [VM] * 11,
        2 * 10**9,
        10**7,
        scratch=[pltpu.VMEM((ROWS, D), BF)],
        limit=30,
    )(pos, pieces, *operands)
    arrived = exchange(parts, ("x", "yl"), TEN)
    summed = call(unsort_kernel, sds((EXP * BLK, 128)), [VM], 10**9, 10**7)(arrived)
    back = exchange(summed, ("z", "yh"), EXP)
    out_t = call(combine_kernel, sds((FEAT, TOK)), [SM, VM, VM], 10**9, 10**6)(pos, back, target)
    return out_t.T


def solution(mesh):
    grid = Mesh(mesh.devices.reshape(8, 4, 2, 4, 2), ("z", "yh", "core", "x", "yl"))
    ex, te = ("z", "yh", "core"), ("x", "yl")
    return jax.shard_map(
        shards,
        mesh=grid,
        in_specs=(P(ex, te), P(ex, None), P(ex, None)) + (P(ex + te, None),) * 5,
        out_specs=P(ex, te),
        check_vma=False,
    )
```

```python
import jax
import jax.numpy as jnp
from jax import lax
from jax.experimental import pallas as pl
from jax.experimental.pallas import tpu as pltpu
from jax.sharding import Mesh, PartitionSpec as P

CAP = 10
HALF = CAP // 2
BLK = 40
EXP = 32
TEN = 8
BIG = 62 * 10**6
SMALL = 16 * 10**6
TOK = 128
FEAT = 448
FULL = 384
FF = 152
D = 3584
PAIR = 2 * FEAT
ROWS = EXP * CAP
HROWS = ROWS // 2
PIECE = 7 * HROWS
GRP = EXP // 2

BF = jnp.bfloat16
F32 = jnp.float32
VM = pl.BlockSpec(memory_space=pltpu.VMEM)
SM = pl.BlockSpec(memory_space=pltpu.SMEM)
HB = pl.BlockSpec(memory_space=pltpu.HBM)


def nt(a, b):
    return lax.dot_general(a, b, (((1,), (1,)), ((), ())), preferred_element_type=F32)


def tn(a, b):
    return lax.dot_general(a, b, (((0,), (0,)), ((), ())), preferred_element_type=F32)


def block_ids():
    e = lax.broadcasted_iota(jnp.int32, (EXP, BLK, TOK), 0).reshape(EXP * BLK, TOK)
    k = lax.broadcasted_iota(jnp.int32, (EXP, BLK, TOK), 1).reshape(EXP * BLK, TOK)
    return e, k


def slots_of(e, k):
    tens = jnp.where(k >= 30, 30, jnp.where(k >= 20, 20, jnp.where(k >= 10, 10, 0)))
    low = jnp.where(k < 35, e * CAP + k - tens, -1)
    high = jnp.where((k >= 30) & (k < 35), e * CAP + k - 30 + HALF, -1)
    return low, high


def fetch(pairs, sems):
    copies = [pltpu.make_async_copy(src, dst, sems.at[i]) for i, (src, dst) in enumerate(pairs)]
    for copy in copies:
        copy.start()
    return copies


def pack_kernel(pos_ref, xt_hbm, gt_hbm, et_hbm, out_ref, tgt_ref, xt_ref, gt_ref, et_ref, sems):
    yl = pos_ref[1]
    for copy in fetch(((xt_hbm, xt_ref), (gt_hbm, gt_ref), (et_hbm, et_ref)), sems):
        copy.wait()
    e0 = et_ref[0:1, :]
    e1 = et_ref[1:2, :]
    xi = lax.broadcasted_iota(jnp.int32, (EXP, TOK), 0)
    named = ((xi == e0) | (xi == e1)).astype(F32).astype(BF)
    earlier = (
        lax.broadcasted_iota(jnp.int32, (TOK, TOK), 0) < lax.broadcasted_iota(jnp.int32, (TOK, TOK), 1)
    ).astype(F32).astype(BF)
    before = jnp.dot(named, earlier, preferred_element_type=F32)
    s0 = jnp.sum(jnp.where(xi == e0, before, 0.0), axis=0, keepdims=True).astype(jnp.int32)
    s1 = jnp.sum(jnp.where(xi == e1, before, 0.0), axis=0, keepdims=True).astype(jnp.int32)
    t0 = e0 * CAP + s0
    t1 = e1 * CAP + s1
    tgt_ref[0:1, :] = t0
    tgt_ref[1:2, :] = t1
    e, k = block_ids()
    low, high = slots_of(e, k)
    one = lambda hit: hit.astype(F32).astype(BF)
    m_low = jnp.concatenate([one(low == t0), one(low == t1)], axis=1)
    m_high = jnp.concatenate([one(high == t0), one(high == t1)], axis=1)

    def scaled(rows):
        x = rows.astype(F32)
        return jnp.concatenate([(x * gt_ref[0:1, :]).astype(BF), (x * gt_ref[1:2, :]).astype(BF)], axis=1)

    full = scaled(xt_ref[pl.ds(pl.multiple_of(64 * yl, 64), FULL), :])
    half = scaled(xt_ref[pl.ds(pl.multiple_of(FULL * (1 - yl), 64), 64), :])
    none = jnp.zeros_like(half)
    wide = nt(m_low, full)
    pair = nt(m_low, jnp.concatenate([half, none], axis=0)) + nt(m_high, jnp.concatenate([none, half], axis=0))
    picked = jnp.where(
        k < 10, wide[:, 0:128], jnp.where(k < 20, wide[:, 128:256], jnp.where(k < 30, wide[:, 256:384], pair))
    )
    out_ref[...] = picked.astype(BF)


def sort_kernel(in_ref, out_hbm, own_ref, sems):
    n_in, rows = GRP * BLK, GRP * HALF
    q = lax.broadcasted_iota(jnp.int32, (rows, n_in), 0)
    col = lax.broadcasted_iota(jnp.int32, (rows, n_in), 1)
    gap = col - 35 * ((q * 205) >> 10) - q
    moves = jnp.concatenate([(gap == HALF * b).astype(F32).astype(BF) for b in range(7)], axis=0)
    both = jnp.concatenate([in_ref[0:n_in, :], in_ref[n_in : 2 * n_in, :]], axis=1)
    res = jnp.dot(moves, both, preferred_element_type=F32).astype(BF)
    for b in range(7):
        for g in range(2):
            at = b * HROWS + g * rows
            own_ref[at : at + rows, :] = res[b * rows : (b + 1) * rows, g * 128 : (g + 1) * 128]
    for copy in fetch([(own_ref, out_hbm.at[pl.ds(t * PIECE, PIECE), :]) for t in range(TEN)], sems):
        copy.wait()


def main_kernel(pos_ref, in_hbm, *refs):
    hbm, out_hbm = refs[0:10], refs[10]
    in_ref, r_ref, out_ref = refs[11:14]
    vmem, sems, out_sems = refs[14:24], refs[24], refs[25]
    core = pos_ref[2]
    piece = lambda ref, t: ref.at[pl.ds(t * PIECE, PIECE), :]
    copies = fetch(
        [(piece(in_hbm, t), piece(in_ref, t)) for t in range(TEN)] + list(zip(hbm, vmem)),
        sems,
    )
    n_col = 2 * ROWS
    row = lax.broadcasted_iota(jnp.int32, (n_col, ROWS), 0)
    r = lax.broadcasted_iota(jnp.int32, (n_col, ROWS), 1)
    h = (r >= HROWS).astype(jnp.int32)
    q = r - HROWS * h
    pick = (row == 15 * ((q * 205) >> 10) + q + HALF * h + CAP * core).astype(F32).astype(BF)
    for i in range(4):
        copies[2 * i].wait()
        copies[2 * i + 1].wait()
        base, even, odd = i * PAIR, 2 * i * PIECE, (2 * i + 1) * PIECE
        for j in range(3):
            r_ref[:, base + 128 * j : base + 128 * (j + 1)] = in_ref[even + j * ROWS : even + (j + 1) * ROWS, :]
            at = base + 512 + 128 * j
            r_ref[:, at : at + 128] = in_ref[odd + j * ROWS : odd + (j + 1) * ROWS, :]
        eh = in_ref[even + 3 * ROWS : even + PIECE, :]
        oh = in_ref[odd + 3 * ROWS : odd + PIECE, :]
        r_ref[0:HROWS, base + FULL : base + 512] = jnp.concatenate([eh[:, :64], oh[:, :64]], axis=1)
        r_ref[HROWS:ROWS, base + FULL : base + 512] = jnp.concatenate([eh[:, 64:], oh[:, 64:]], axis=1)

    grads = []
    for i in range(2):
        wd, sg, su, wg, wu = vmem[5 * i : 5 * i + 5]
        for k in range(3):
            copies[TEN + 5 * i + k].wait()
        hidden = nt(wd[...], r_ref[...])
        g = jnp.dot(sg[...], pick, preferred_element_type=F32)
        u = jnp.dot(su[...], pick, preferred_element_type=F32)
        sig = 1.0 / (1.0 + jnp.exp(-g))
        gate = hidden * u * sig * (1.0 + g * (1.0 - sig))
        up = hidden * g * sig
        grads.append((gate.T.astype(BF), wg))
        grads.append((up.T.astype(BF), wu))
    for k in (3, 4, 8, 9):
        copies[TEN + k].wait()

    back = []
    for i in range(4):
        base, even, odd = i * PAIR, 2 * i * PIECE, (2 * i + 1) * PIECE
        acc = None
        for grad, w in grads:
            term = jnp.dot(grad, w[:, base : base + PAIR], preferred_element_type=F32)
            acc = term if acc is None else acc + term
        acc = acc.astype(BF)
        for j in range(3):
            out_ref[even + j * ROWS : even + (j + 1) * ROWS, :] = acc[:, 128 * j : 128 * (j + 1)]
            out_ref[odd + j * ROWS : odd + (j + 1) * ROWS, :] = acc[:, 512 + 128 * j : 512 + 128 * (j + 1)]
        lo = acc[0:HROWS, FULL:512]
        hi = acc[HROWS:ROWS, FULL:512]
        out_ref[even + 3 * ROWS : even + PIECE, :] = jnp.concatenate([lo[:, :64], hi[:, :64]], axis=1)
        out_ref[odd + 3 * ROWS : odd + PIECE, :] = jnp.concatenate([lo[:, 64:], hi[:, 64:]], axis=1)
        for t in (2 * i, 2 * i + 1):
            copy = pltpu.make_async_copy(piece(out_ref, t), piece(out_hbm, t), out_sems.at[t])
            copy.start()
            back.append(copy)
    for copy in back:
        copy.wait()


def unsort_kernel(in_ref, out_ref):
    rows = GRP * HALF
    n_out = GRP * BLK
    q = lax.broadcasted_iota(jnp.int32, (n_out, rows), 1)
    row = lax.broadcasted_iota(jnp.int32, (n_out, rows), 0)
    gap = row - 35 * ((q * 205) >> 10) - q
    res = [None, None]
    for b in range(7):
        move = (gap == HALF * b).astype(F32).astype(BF)
        cols = []
        for g in range(2):
            total = None
            for t in range(TEN):
                at = t * PIECE + b * HROWS + g * rows
                part = in_ref[at : at + rows, :].astype(F32)
                total = part if total is None else total + part
            cols.append(total.astype(BF))
        term = jnp.dot(move, jnp.concatenate(cols, axis=1), preferred_element_type=F32)
        for g in range(2):
            t = term[:, g * 128 : (g + 1) * 128]
            res[g] = t if res[g] is None else res[g] + t
    for g in range(2):
        out_ref[g * n_out : (g + 1) * n_out, :] = res[g].astype(BF)


def combine_kernel(pos_ref, in_ref, tgt_ref, out_ref):
    yl = pos_ref[1]
    t0 = tgt_ref[0:1, :]
    t1 = tgt_ref[1:2, :]
    e, k = block_ids()
    low, high = slots_of(e, k)
    hit = ((low == t0) | (low == t1)).astype(F32)
    cut = lambda a, b: jnp.where((k >= a) & (k < b), hit, 0.0).astype(BF)
    hit_high = ((high == t0) | (high == t1)).astype(F32).astype(BF)
    take = jnp.concatenate([cut(0, 10), cut(10, 20), cut(20, 30), cut(30, 35), hit_high], axis=1)
    res = tn(in_ref[...], take)
    start = pl.multiple_of(64 * yl, 64)
    for j in range(3):
        out_ref[pl.ds(pl.multiple_of(start + 128 * j, 64), 128), :] = res[:, 128 * j : 128 * (j + 1)].astype(BF)
    half = res[0:64, FULL:512] + res[64:128, 512:640]
    out_ref[pl.ds(pl.multiple_of(FULL * (1 - yl), 64), 64), :] = half.astype(BF)


def call(kernel, outs, specs, flops=0, moved=0, scratch=(), limit=BIG, out_spec=VM):
    many = isinstance(outs, (list, tuple))
    return pl.pallas_call(
        kernel,
        out_shape=outs,
        in_specs=specs,
        out_specs=[out_spec] * len(outs) if many else out_spec,
        scratch_shapes=list(scratch),
        cost_estimate=pl.CostEstimate(flops=flops, bytes_accessed=moved, transcendentals=0),
        compiler_params=pltpu.CompilerParams(vmem_limit_bytes=limit),
    )


def sds(shape, dtype=BF):
    return jax.ShapeDtypeStruct(shape, dtype)


def swap_core(a):
    return lax.ppermute(a, "core", [(0, 1), (1, 0)])


def exchange(a, axes, n):
    blocks = a.reshape(n, a.shape[0] // n, a.shape[1])
    return lax.all_to_all(blocks, axes, split_axis=0, concat_axis=0, tiled=True).reshape(a.shape)


def shards(out_grad, gate_probs, expert_ids, saved_gate, saved_up, w_gate, w_up, w_down):
    pos = jnp.stack([lax.axis_index("x"), lax.axis_index("yl"), lax.axis_index("core")]).astype(jnp.int32)
    dma = pltpu.SemaphoreType.DMA
    packed, target = call(
        pack_kernel,
        [sds((EXP * BLK, 128)), sds((2, TOK), jnp.int32)],
        [SM, HB, HB, HB],
        10**9,
        10**6,
        scratch=[
            pltpu.VMEM((FEAT, TOK), BF),
            pltpu.VMEM((2, TOK), F32),
            pltpu.VMEM((2, TOK), jnp.int32),
            dma((3,)),
        ],
    )(pos, out_grad.T, gate_probs.T, expert_ids.T)
    got = exchange(packed, ("z", "yh"), EXP)
    spread = call(
        sort_kernel,
        sds((TEN * PIECE, 128)),
        [VM],
        10**9,
        10**6,
        scratch=[pltpu.VMEM((PIECE, 128), BF), dma((TEN,))],
        out_spec=HB,
    )(got)
    pieces = exchange(spread, ("x", "yl"), TEN)
    own = [w_down, saved_gate, saved_up, w_gate, w_up]
    operands = own + [swap_core(a) for a in own]
    parts = call(
        main_kernel,
        sds((TEN * PIECE, 128)),
        [SM] + [HB] * 11,
        2 * 10**9,
        10**7,
        scratch=[pltpu.VMEM((TEN * PIECE, 128), BF), pltpu.VMEM((ROWS, D), BF), pltpu.VMEM((TEN * PIECE, 128), BF)]
        + [pltpu.VMEM(a.shape, BF) for a in operands]
        + [dma((TEN + 10,)), dma((TEN,))],
        out_spec=HB,
    )(pos, pieces, *operands)
    arrived = exchange(parts, ("x", "yl"), TEN)
    summed = call(unsort_kernel, sds((EXP * BLK, 128)), [VM], 10**9, 10**7, limit=SMALL)(arrived)
    back = exchange(summed, ("z", "yh"), EXP)
    out_t = call(combine_kernel, sds((FEAT, TOK)), [SM, VM, VM], 10**9, 10**6, limit=SMALL)(
        pos, back, target
    )
    return out_t.T


def solution(mesh):
    grid = Mesh(mesh.devices.reshape(8, 4, 2, 4, 2), ("z", "yh", "core", "x", "yl"))
    ex, te = ("z", "yh", "core"), ("x", "yl")
    return jax.shard_map(
        shards,
        mesh=grid,
        in_specs=(P(ex, te), P(ex, None), P(ex, None)) + (P(ex + te, None),) * 5,
        out_specs=P(ex, te),
        check_vma=False,
    )
```

```python
import jax
import jax.numpy as jnp
from jax import lax
from jax.experimental import pallas as pl
from jax.experimental.pallas import tpu as pltpu
from jax.sharding import Mesh, PartitionSpec as P

CAP = 10
HALF = CAP // 2
BLK = 40
EXP = 32
TEN = 8
BIG = 62 * 10**6
MID = 57 * 10**6
SMALL = 16 * 10**6
TOK = 128
FEAT = 448
FULL = 384
FF = 152
PAIR = 2 * FEAT
ROWS = EXP * CAP
HROWS = ROWS // 2
PIECE = 7 * HROWS
GRP = EXP // 2
FPAD = 160
D = 3584

BF = jnp.bfloat16
F32 = jnp.float32
VM = pl.BlockSpec(memory_space=pltpu.VMEM)
AN = pl.BlockSpec(memory_space=pl.ANY)


def nt(a, b):
    return lax.dot_general(a, b, (((1,), (1,)), ((), ())), preferred_element_type=F32)


def tn(a, b):
    return lax.dot_general(a, b, (((0,), (0,)), ((), ())), preferred_element_type=F32)


def block_ids(rows=BLK):
    e = lax.broadcasted_iota(jnp.int32, (EXP, rows, TOK), 0).reshape(EXP * rows, TOK)
    k = lax.broadcasted_iota(jnp.int32, (EXP, rows, TOK), 1).reshape(EXP * rows, TOK)
    return e, k


def slots_of(e, k):
    tens = jnp.where(k >= 30, 30, jnp.where(k >= 20, 20, jnp.where(k >= 10, 10, 0)))
    low = jnp.where(k < 35, e * CAP + k - tens, -1)
    high = jnp.where((k >= 30) & (k < 35), e * CAP + k - 30 + HALF, -1)
    return low, high


def pack_kernel(xt_ref, gt_ref, et_ref, out_ref, tgt_ref):
    yl = lax.axis_index("yl")
    e0 = et_ref[0:1, :]
    e1 = et_ref[1:2, :]
    xi = lax.broadcasted_iota(jnp.int32, (EXP, TOK), 0)
    named = ((xi == e0) | (xi == e1)).astype(F32).astype(BF)
    earlier = (
        lax.broadcasted_iota(jnp.int32, (TOK, TOK), 0) < lax.broadcasted_iota(jnp.int32, (TOK, TOK), 1)
    ).astype(F32).astype(BF)
    before = jnp.dot(named, earlier, preferred_element_type=F32)
    s0 = jnp.sum(jnp.where(xi == e0, before, 0.0), axis=0, keepdims=True).astype(jnp.int32)
    s1 = jnp.sum(jnp.where(xi == e1, before, 0.0), axis=0, keepdims=True).astype(jnp.int32)
    t0 = e0 * CAP + s0
    t1 = e1 * CAP + s1
    tgt_ref[0:1, :] = t0
    tgt_ref[1:2, :] = t1
    e, k = block_ids()
    low, high = slots_of(e, k)
    one = lambda hit: hit.astype(F32).astype(BF)
    m_low = jnp.concatenate([one(low == t0), one(low == t1)], axis=1)
    m_high = jnp.concatenate([one(high == t0), one(high == t1)], axis=1)

    def scaled(rows):
        x = rows.astype(F32)
        return jnp.concatenate([(x * gt_ref[0:1, :]).astype(BF), (x * gt_ref[1:2, :]).astype(BF)], axis=1)

    full = scaled(xt_ref[pl.ds(pl.multiple_of(64 * yl, 64), FULL), :])
    half = scaled(xt_ref[pl.ds(pl.multiple_of(FULL * (1 - yl), 64), 64), :])
    none = jnp.zeros_like(half)
    wide = nt(m_low, full)
    pair = nt(m_low, jnp.concatenate([half, none], axis=0)) + nt(m_high, jnp.concatenate([none, half], axis=0))
    picked = jnp.where(
        k < 10, wide[:, 0:128], jnp.where(k < 20, wide[:, 128:256], jnp.where(k < 30, wide[:, 256:384], pair))
    )
    out_ref[...] = picked.astype(BF)


def sort_kernel(in_ref, out_ref):
    n_in, rows = GRP * BLK, GRP * HALF
    q = lax.broadcasted_iota(jnp.int32, (rows, n_in), 0)
    col = lax.broadcasted_iota(jnp.int32, (rows, n_in), 1)
    gap = col - 35 * ((q * 205) >> 10) - q
    moves = jnp.concatenate([(gap == HALF * b).astype(F32).astype(BF) for b in range(7)], axis=0)
    both = jnp.concatenate([in_ref[0:n_in, :], in_ref[n_in : 2 * n_in, :]], axis=1)
    res = jnp.dot(moves, both, preferred_element_type=F32).astype(BF)
    for b in range(7):
        for g in range(2):
            block = res[b * rows : (b + 1) * rows, g * 128 : (g + 1) * 128]
            for t in range(TEN):
                at = t * PIECE + b * HROWS + g * rows
                out_ref[at : at + rows, :] = block


def stack_kernel(wd0, wd1, wg0, wg1, wu0, wu1, sg0, sg1, su0, su1, w_ref, f_ref, sg_ref, su_ref):
    def stack(ref, first, blocks):
        for i, block in enumerate(blocks):
            at = first + i * FPAD
            ref[at + FPAD - 16 : at + FPAD, :] = jnp.zeros((16, ref.shape[1]), BF)
            ref[at : at + FF, :] = block[...]

    stack(w_ref, 0, (wd0, wd1, wg0, wg1, wu0, wu1))

    @pl.when(pl.program_id(0) == 0)
    def _():
        stack(sg_ref, 0, (sg0, sg1))
        stack(su_ref, 0, (su0, su1))
        core = lax.axis_index("core")
        r = lax.broadcasted_iota(jnp.int32, (ROWS, 2 * ROWS), 0)
        col = lax.broadcasted_iota(jnp.int32, (ROWS, 2 * ROWS), 1)
        h = (r >= HROWS).astype(jnp.int32)
        q = r - HROWS * h
        pick = (col == 15 * ((q * 205) >> 10) + q + HALF * h + CAP * core).astype(F32).astype(BF)
        g = nt(pick, sg_ref[...])
        u = nt(pick, su_ref[...])
        sig = 1.0 / (1.0 + jnp.exp(-g))
        f_ref[0] = u * sig * (1.0 + g * (1.0 - sig))
        f_ref[1] = g * sig


def main_kernel(in_ref, f_ref, w_hbm, out_ref, r_ref, w_ref, sems):
    down, rest = 2 * FPAD, 4 * FPAD
    copies = [
        pltpu.make_async_copy(w_hbm.at[pl.ds(at, n), :], w_ref.at[pl.ds(at, n), :], sems.at[i])
        for i, (at, n) in enumerate(((0, down), (down, rest)))
    ]
    for copy in copies:
        copy.start()
    for i in range(4):
        base, even, odd = i * PAIR, 2 * i * PIECE, (2 * i + 1) * PIECE
        for j in range(3):
            r_ref[:, base + 128 * j : base + 128 * (j + 1)] = in_ref[even + j * ROWS : even + (j + 1) * ROWS, :]
            at = base + 512 + 128 * j
            r_ref[:, at : at + 128] = in_ref[odd + j * ROWS : odd + (j + 1) * ROWS, :]
        eh = in_ref[even + 3 * ROWS : even + PIECE, :]
        oh = in_ref[odd + 3 * ROWS : odd + PIECE, :]
        r_ref[0:HROWS, base + FULL : base + 512] = jnp.concatenate([eh[:, :64], oh[:, :64]], axis=1)
        r_ref[HROWS:ROWS, base + FULL : base + 512] = jnp.concatenate([eh[:, 64:], oh[:, 64:]], axis=1)
    copies[0].wait()
    hidden = nt(r_ref[...], w_ref[0:down, :])
    grads = jnp.concatenate([hidden * f_ref[0], hidden * f_ref[1]], axis=1).astype(BF)
    copies[1].wait()
    for i in range(4):
        base, even, odd = i * PAIR, 2 * i * PIECE, (2 * i + 1) * PIECE
        acc = jnp.dot(grads, w_ref[down:, base : base + PAIR], preferred_element_type=F32).astype(BF)
        for j in range(3):
            out_ref[even + j * ROWS : even + (j + 1) * ROWS, :] = acc[:, 128 * j : 128 * (j + 1)]
            out_ref[odd + j * ROWS : odd + (j + 1) * ROWS, :] = acc[:, 512 + 128 * j : 512 + 128 * (j + 1)]
        lo = acc[0:HROWS, FULL:512]
        hi = acc[HROWS:ROWS, FULL:512]
        out_ref[even + 3 * ROWS : even + PIECE, :] = jnp.concatenate([lo[:, :64], hi[:, :64]], axis=1)
        out_ref[odd + 3 * ROWS : odd + PIECE, :] = jnp.concatenate([lo[:, 64:], hi[:, 64:]], axis=1)


def unsort_kernel(in_ref, out_ref):
    rows = GRP * HALF
    n_out = GRP * BLK
    q = lax.broadcasted_iota(jnp.int32, (n_out, rows), 1)
    row = lax.broadcasted_iota(jnp.int32, (n_out, rows), 0)
    gap = row - 35 * ((q * 205) >> 10) - q
    res = [None, None]
    for b in range(7):
        move = (gap == HALF * b).astype(F32).astype(BF)
        cols = []
        for g in range(2):
            total = None
            for t in range(TEN):
                at = t * PIECE + b * HROWS + g * rows
                part = in_ref[at : at + rows, :].astype(F32)
                total = part if total is None else total + part
            cols.append(total.astype(BF))
        term = jnp.dot(move, jnp.concatenate(cols, axis=1), preferred_element_type=F32)
        for g in range(2):
            t = term[:, g * 128 : (g + 1) * 128]
            res[g] = t if res[g] is None else res[g] + t
    for g in range(2):
        out_ref[g * n_out : (g + 1) * n_out, :] = res[g].astype(BF)


def combine_kernel(in_ref, tgt_ref, out_ref):
    yl = lax.axis_index("yl")
    t0 = tgt_ref[0:1, :]
    t1 = tgt_ref[1:2, :]
    e, k = block_ids()
    low, high = slots_of(e, k)
    hit = ((low == t0) | (low == t1)).astype(F32)
    cut = lambda a, b: jnp.where((k >= a) & (k < b), hit, 0.0).astype(BF)
    hit_high = ((high == t0) | (high == t1)).astype(F32).astype(BF)
    take = jnp.concatenate([cut(0, 10), cut(10, 20), cut(20, 30), cut(30, 35), hit_high], axis=1)
    res = tn(in_ref[...], take)
    start = pl.multiple_of(64 * yl, 64)
    for j in range(3):
        out_ref[pl.ds(pl.multiple_of(start + 128 * j, 64), 128), :] = res[:, 128 * j : 128 * (j + 1)].astype(BF)
    half = res[0:64, FULL:512] + res[64:128, 512:640]
    out_ref[pl.ds(pl.multiple_of(FULL * (1 - yl), 64), 64), :] = half.astype(BF)


def call(kernel, outs, specs, flops, moved, scratch=(), limit=SMALL, grid=(), out_specs=VM):
    if isinstance(outs, list) and not isinstance(out_specs, list):
        out_specs = [out_specs] * len(outs)
    return pl.pallas_call(
        kernel,
        out_shape=outs,
        grid=grid,
        in_specs=specs,
        out_specs=out_specs,
        scratch_shapes=list(scratch),
        cost_estimate=pl.CostEstimate(flops=flops, bytes_accessed=moved, transcendentals=0),
        compiler_params=pltpu.CompilerParams(vmem_limit_bytes=limit),
    )


def sds(shape, dtype=BF):
    return jax.ShapeDtypeStruct(shape, dtype)


def swap_core(a):
    return lax.ppermute(a, "core", [(0, 1), (1, 0)])


def exchange(a, axes, n):
    blocks = a.reshape(n, a.shape[0] // n, a.shape[1])
    return lax.all_to_all(blocks, axes, split_axis=0, concat_axis=0, tiled=True).reshape(a.shape)


def shards(out_grad, gate_probs, expert_ids, saved_gate, saved_up, w_gate, w_up, w_down):
    packed, target = call(
        pack_kernel,
        [sds((EXP * BLK, 128)), sds((2, TOK), jnp.int32)],
        [VM, VM, VM],
        10**9,
        10**6,
        limit=BIG,
    )(out_grad.T, gate_probs.T, expert_ids.T)
    got = exchange(packed, ("z", "yh"), EXP)
    spread = call(sort_kernel, sds((TEN * PIECE, 128)), [VM], 10**9, 3 * 10**6)(got)
    pieces = exchange(spread, ("x", "yl"), TEN)

    operands = []
    for a in (w_down, w_gate, w_up, saved_gate, saved_up):
        operands += [a, swap_core(a)]
    block = pl.BlockSpec((FF, PAIR), lambda i: (0, i))
    saved = pl.BlockSpec((FF, 2 * ROWS), lambda i: (0, 0))
    weights, factors = call(
        stack_kernel,
        [sds((6 * FPAD, D)), sds((2, ROWS, 2 * FPAD), F32)],
        [block] * 6 + [saved] * 4,
        5 * 10**8,
        16 * 10**6,
        scratch=[pltpu.VMEM((2 * FPAD, 2 * ROWS), BF)] * 2,
        limit=BIG,
        grid=(4,),
        out_specs=[
            pl.BlockSpec((6 * FPAD, PAIR), lambda i: (0, i)),
            pl.BlockSpec((2, ROWS, 2 * FPAD), lambda i: (0, 0, 0)),
        ],
    )(*operands)
    parts = call(
        main_kernel,
        sds((TEN * PIECE, 128)),
        [VM, VM, AN],
        23 * 10**8,
        12 * 10**6,
        scratch=[pltpu.VMEM((ROWS, D), BF), pltpu.VMEM((6 * FPAD, D), BF), pltpu.SemaphoreType.DMA((2,))],
        limit=MID,
    )(pieces, factors, weights)
    home = exchange(parts, ("x", "yl"), TEN)
    summed = call(unsort_kernel, sds((EXP * BLK, 128)), [VM], 10**9, 3 * 10**6)(home)
    back = exchange(summed, ("z", "yh"), EXP)
    out_t = call(combine_kernel, sds((FEAT, TOK)), [VM, VM], 10**9, 10**6)(back, target)
    return out_t.T


def solution(mesh):
    grid = Mesh(mesh.devices.reshape(8, 4, 2, 4, 2), ("z", "yh", "core", "x", "yl"))
    ex, te = ("z", "yh", "core"), ("x", "yl")
    return jax.shard_map(
        shards,
        mesh=grid,
        in_specs=(P(ex, te), P(ex, None), P(ex, None)) + (P(ex + te, None),) * 5,
        out_specs=P(ex, te),
        check_vma=False,
    )
```

```python
import jax
import jax.numpy as jnp
from jax import lax
from jax.experimental import pallas as pl
from jax.experimental.pallas import tpu as pltpu
from jax.sharding import Mesh, PartitionSpec as P

CAP = 10
HALF = CAP // 2
BLK = 40
EXP = 32
TEN = 8
BIG = 62 * 10**6
MID = 50 * 10**6
SMALL = 16 * 10**6
TOK = 128
FEAT = 448
FULL = 384
FF = 152
PAIR = 2 * FEAT
ROWS = EXP * CAP
HROWS = ROWS // 2
PIECE = 7 * HROWS
GRP = EXP // 2
FPAD = 160
D = 3584

BF = jnp.bfloat16
F32 = jnp.float32
VM = pl.BlockSpec(memory_space=pltpu.VMEM)
AN = pl.BlockSpec(memory_space=pl.ANY)


def nt(a, b):
    return lax.dot_general(a, b, (((1,), (1,)), ((), ())), preferred_element_type=F32)


def tn(a, b):
    return lax.dot_general(a, b, (((0,), (0,)), ((), ())), preferred_element_type=F32)


def block_ids(rows=BLK):
    e = lax.broadcasted_iota(jnp.int32, (EXP, rows, TOK), 0).reshape(EXP * rows, TOK)
    k = lax.broadcasted_iota(jnp.int32, (EXP, rows, TOK), 1).reshape(EXP * rows, TOK)
    return e, k


def slots_of(e, k):
    tens = jnp.where(k >= 30, 30, jnp.where(k >= 20, 20, jnp.where(k >= 10, 10, 0)))
    low = jnp.where(k < 35, e * CAP + k - tens, -1)
    high = jnp.where((k >= 30) & (k < 35), e * CAP + k - 30 + HALF, -1)
    return low, high


def pack_kernel(xt_ref, gt_ref, et_ref, out_ref, tgt_ref):
    yl = lax.axis_index("yl")
    e0 = et_ref[0:1, :]
    e1 = et_ref[1:2, :]
    xi = lax.broadcasted_iota(jnp.int32, (EXP, TOK), 0)
    named = ((xi == e0) | (xi == e1)).astype(F32).astype(BF)
    earlier = (
        lax.broadcasted_iota(jnp.int32, (TOK, TOK), 0) < lax.broadcasted_iota(jnp.int32, (TOK, TOK), 1)
    ).astype(F32).astype(BF)
    before = jnp.dot(named, earlier, preferred_element_type=F32)
    s0 = jnp.sum(jnp.where(xi == e0, before, 0.0), axis=0, keepdims=True).astype(jnp.int32)
    s1 = jnp.sum(jnp.where(xi == e1, before, 0.0), axis=0, keepdims=True).astype(jnp.int32)
    t0 = e0 * CAP + s0
    t1 = e1 * CAP + s1
    tgt_ref[0:1, :] = t0
    tgt_ref[1:2, :] = t1
    e, k = block_ids()
    low, high = slots_of(e, k)
    one = lambda hit: hit.astype(F32).astype(BF)
    m_low = jnp.concatenate([one(low == t0), one(low == t1)], axis=1)
    m_high = jnp.concatenate([one(high == t0), one(high == t1)], axis=1)

    def scaled(rows):
        x = rows.astype(F32)
        return jnp.concatenate([(x * gt_ref[0:1, :]).astype(BF), (x * gt_ref[1:2, :]).astype(BF)], axis=1)

    full = scaled(xt_ref[pl.ds(pl.multiple_of(64 * yl, 64), FULL), :])
    half = scaled(xt_ref[pl.ds(pl.multiple_of(FULL * (1 - yl), 64), 64), :])
    none = jnp.zeros_like(half)
    wide = nt(m_low, full)
    pair = nt(m_low, jnp.concatenate([half, none], axis=0)) + nt(m_high, jnp.concatenate([none, half], axis=0))
    picked = jnp.where(
        k < 10, wide[:, 0:128], jnp.where(k < 20, wide[:, 128:256], jnp.where(k < 30, wide[:, 256:384], pair))
    )
    out_ref[...] = picked.astype(BF)


def sort_kernel(in_ref, out_ref):
    n_in, rows = GRP * BLK, GRP * HALF
    q = lax.broadcasted_iota(jnp.int32, (rows, n_in), 0)
    col = lax.broadcasted_iota(jnp.int32, (rows, n_in), 1)
    gap = col - 35 * ((q * 205) >> 10) - q
    moves = jnp.concatenate([(gap == HALF * b).astype(F32).astype(BF) for b in range(7)], axis=0)
    both = jnp.concatenate([in_ref[0:n_in, :], in_ref[n_in : 2 * n_in, :]], axis=1)
    res = jnp.dot(moves, both, preferred_element_type=F32).astype(BF)
    for b in range(7):
        for g in range(2):
            block = res[b * rows : (b + 1) * rows, g * 128 : (g + 1) * 128]
            for t in range(TEN):
                at = t * PIECE + b * HROWS + g * rows
                out_ref[at : at + rows, :] = block


def stack_kernel(wd0, wd1, wg0, wg1, wu0, wu1, sg0, sg1, su0, su1, w_ref, f_ref, sg_ref, su_ref):
    def stack(ref, first, blocks):
        for i, block in enumerate(blocks):
            at = first + i * FPAD
            ref[at + FPAD - 16 : at + FPAD, :] = jnp.zeros((16, ref.shape[1]), BF)
            ref[at : at + FF, :] = block[...]

    stack(w_ref, 0, (wd0, wd1, wg0, wg1, wu0, wu1))

    @pl.when(pl.program_id(0) == 0)
    def _():
        stack(sg_ref, 0, (sg0, sg1))
        stack(su_ref, 0, (su0, su1))
        core = lax.axis_index("core")
        r = lax.broadcasted_iota(jnp.int32, (ROWS, 2 * ROWS), 0)
        col = lax.broadcasted_iota(jnp.int32, (ROWS, 2 * ROWS), 1)
        h = (r >= HROWS).astype(jnp.int32)
        q = r - HROWS * h
        pick = (col == 15 * ((q * 205) >> 10) + q + HALF * h + CAP * core).astype(F32).astype(BF)
        g = nt(pick, sg_ref[...])
        u = nt(pick, su_ref[...])
        sig = 1.0 / (1.0 + jnp.exp(-g))
        f_ref[0] = u * sig * (1.0 + g * (1.0 - sig))
        f_ref[1] = g * sig


def main_kernel(in_ref, f_ref, w_hbm, out_ref, r_ref, w_ref, sems):
    down, rest = 2 * FPAD, 4 * FPAD
    copies = [
        pltpu.make_async_copy(w_hbm.at[pl.ds(at, n), :], w_ref.at[pl.ds(at, n), :], sems.at[i])
        for i, (at, n) in enumerate(((0, down), (down, rest)))
    ]
    for copy in copies:
        copy.start()
    for i in range(4):
        base, even, odd = i * PAIR, i * PIECE, (4 + i) * PIECE
        for j in range(3):
            r_ref[:, base + 128 * j : base + 128 * (j + 1)] = in_ref[even + j * ROWS : even + (j + 1) * ROWS, :]
            at = base + 512 + 128 * j
            r_ref[:, at : at + 128] = in_ref[odd + j * ROWS : odd + (j + 1) * ROWS, :]
        eh = in_ref[even + 3 * ROWS : even + PIECE, :]
        oh = in_ref[odd + 3 * ROWS : odd + PIECE, :]
        r_ref[0:HROWS, base + FULL : base + 512] = jnp.concatenate([eh[:, :64], oh[:, :64]], axis=1)
        r_ref[HROWS:ROWS, base + FULL : base + 512] = jnp.concatenate([eh[:, 64:], oh[:, 64:]], axis=1)
    copies[0].wait()
    hidden = nt(r_ref[...], w_ref[0:down, :])
    grads = jnp.concatenate([hidden * f_ref[0], hidden * f_ref[1]], axis=1).astype(BF)
    copies[1].wait()
    for i in range(4):
        base, even, odd = i * PAIR, i * PIECE, (4 + i) * PIECE
        acc = jnp.dot(grads, w_ref[down:, base : base + PAIR], preferred_element_type=F32).astype(BF)
        for j in range(3):
            out_ref[even + j * ROWS : even + (j + 1) * ROWS, :] = acc[:, 128 * j : 128 * (j + 1)]
            out_ref[odd + j * ROWS : odd + (j + 1) * ROWS, :] = acc[:, 512 + 128 * j : 512 + 128 * (j + 1)]
        lo = acc[0:HROWS, FULL:512]
        hi = acc[HROWS:ROWS, FULL:512]
        out_ref[even + 3 * ROWS : even + PIECE, :] = jnp.concatenate([lo[:, :64], hi[:, :64]], axis=1)
        out_ref[odd + 3 * ROWS : odd + PIECE, :] = jnp.concatenate([lo[:, 64:], hi[:, 64:]], axis=1)


def unsort_kernel(in_ref, out_ref):
    rows = GRP * HALF
    n_out = GRP * BLK
    q = lax.broadcasted_iota(jnp.int32, (n_out, rows), 1)
    row = lax.broadcasted_iota(jnp.int32, (n_out, rows), 0)
    gap = row - 35 * ((q * 205) >> 10) - q
    res = [None, None]
    for b in range(7):
        move = (gap == HALF * b).astype(F32).astype(BF)
        cols = []
        for g in range(2):
            total = None
            for t in range(TEN):
                at = t * PIECE + b * HROWS + g * rows
                part = in_ref[at : at + rows, :].astype(F32)
                total = part if total is None else total + part
            cols.append(total.astype(BF))
        term = jnp.dot(move, jnp.concatenate(cols, axis=1), preferred_element_type=F32)
        for g in range(2):
            t = term[:, g * 128 : (g + 1) * 128]
            res[g] = t if res[g] is None else res[g] + t
    for g in range(2):
        out_ref[g * n_out : (g + 1) * n_out, :] = res[g].astype(BF)


def combine_kernel(in_ref, tgt_ref, out_ref):
    yl = lax.axis_index("yl")
    t0 = tgt_ref[0:1, :]
    t1 = tgt_ref[1:2, :]
    e, k = block_ids()
    low, high = slots_of(e, k)
    hit = ((low == t0) | (low == t1)).astype(F32)
    cut = lambda a, b: jnp.where((k >= a) & (k < b), hit, 0.0).astype(BF)
    hit_high = ((high == t0) | (high == t1)).astype(F32).astype(BF)
    take = jnp.concatenate([cut(0, 10), cut(10, 20), cut(20, 30), cut(30, 35), hit_high], axis=1)
    res = tn(in_ref[...], take)
    start = pl.multiple_of(64 * yl, 64)
    for j in range(3):
        out_ref[pl.ds(pl.multiple_of(start + 128 * j, 64), 128), :] = res[:, 128 * j : 128 * (j + 1)].astype(BF)
    half = res[0:64, FULL:512] + res[64:128, 512:640]
    out_ref[pl.ds(pl.multiple_of(FULL * (1 - yl), 64), 64), :] = half.astype(BF)


def call(kernel, outs, specs, flops, moved, scratch=(), limit=SMALL, grid=(), out_specs=VM):
    if isinstance(outs, list) and not isinstance(out_specs, list):
        out_specs = [out_specs] * len(outs)
    return pl.pallas_call(
        kernel,
        out_shape=outs,
        grid=grid,
        in_specs=specs,
        out_specs=out_specs,
        scratch_shapes=list(scratch),
        cost_estimate=pl.CostEstimate(flops=flops, bytes_accessed=moved, transcendentals=0),
        compiler_params=pltpu.CompilerParams(vmem_limit_bytes=limit),
    )


def sds(shape, dtype=BF):
    return jax.ShapeDtypeStruct(shape, dtype)


def swap_core(a):
    return lax.ppermute(a, "core", [(0, 1), (1, 0)])


def exchange(a, axes, n):
    blocks = a.reshape(n, a.shape[0] // n, a.shape[1])
    return lax.all_to_all(blocks, axes, split_axis=0, concat_axis=0, tiled=True).reshape(a.shape)


def shards(out_grad, gate_probs, expert_ids, saved_gate, saved_up, w_gate, w_up, w_down):
    packed, target = call(
        pack_kernel,
        [sds((EXP * BLK, 128)), sds((2, TOK), jnp.int32)],
        [VM, VM, VM],
        10**9,
        10**6,
        limit=BIG,
    )(out_grad.T, gate_probs.T, expert_ids.T)
    got = exchange(packed, ("z", "yh"), EXP)
    spread = call(sort_kernel, sds((TEN * PIECE, 128)), [VM], 10**9, 3 * 10**6)(got)
    pieces = exchange(spread, ("yl", "x"), TEN)

    operands = []
    for a in (w_down, w_gate, w_up, saved_gate, saved_up):
        operands += [a, swap_core(a)]
    block = pl.BlockSpec((FF, PAIR), lambda i: (0, i))
    saved = pl.BlockSpec((FF, 2 * ROWS), lambda i: (0, 0))
    weights, factors = call(
        stack_kernel,
        [sds((6 * FPAD, D)), sds((2, ROWS, 2 * FPAD), F32)],
        [block] * 6 + [saved] * 4,
        5 * 10**8,
        16 * 10**6,
        scratch=[pltpu.VMEM((2 * FPAD, 2 * ROWS), BF)] * 2,
        limit=BIG,
        grid=(4,),
        out_specs=[
            pl.BlockSpec((6 * FPAD, PAIR), lambda i: (0, i)),
            pl.BlockSpec((2, ROWS, 2 * FPAD), lambda i: (0, 0, 0)),
        ],
    )(*operands)
    parts = call(
        main_kernel,
        sds((TEN * PIECE, 128)),
        [VM, VM, AN],
        23 * 10**8,
        12 * 10**6,
        scratch=[pltpu.VMEM((ROWS, D), BF), pltpu.VMEM((6 * FPAD, D), BF), pltpu.SemaphoreType.DMA((2,))],
        limit=MID,
    )(pieces, factors, weights)
    home = exchange(parts, ("yl", "x"), TEN)
    summed = call(unsort_kernel, sds((EXP * BLK, 128)), [VM], 10**9, 3 * 10**6)(home)
    back = exchange(summed, ("z", "yh"), EXP)
    out_t = call(combine_kernel, sds((FEAT, TOK)), [VM, VM], 10**9, 10**6)(back, target)
    return out_t.T


def solution(mesh):
    grid = Mesh(mesh.devices.reshape(8, 4, 2, 4, 2), ("z", "yh", "core", "x", "yl"))
    ex, te = ("z", "yh", "core"), ("x", "yl")
    return jax.shard_map(
        shards,
        mesh=grid,
        in_specs=(P(ex, te), P(ex, None), P(ex, None)) + (P(ex + te, None),) * 5,
        out_specs=P(ex, te),
        check_vma=False,
    )
```

```python
import jax
import jax.numpy as jnp
from jax import lax
from jax.experimental import pallas as pl
from jax.experimental.pallas import tpu as pltpu
from jax.sharding import Mesh, PartitionSpec as P

CAP = 10
HALF = CAP // 2
BLK = 40
EXP = 32
TEN = 8
BIG = 62 * 10**6
MID = 50 * 10**6
SMALL = 16 * 10**6
TOK = 128
FEAT = 448
FULL = 384
FF = 152
PAIR = 2 * FEAT
ROWS = EXP * CAP
HROWS = ROWS // 2
PIECE = 7 * HROWS
GRP = EXP // 2
FPAD = 160
D = 3584

BF = jnp.bfloat16
F32 = jnp.float32
VM = pl.BlockSpec(memory_space=pltpu.VMEM)
AN = pl.BlockSpec(memory_space=pl.ANY)


def nt(a, b):
    return lax.dot_general(a, b, (((1,), (1,)), ((), ())), preferred_element_type=F32)


def tn(a, b):
    return lax.dot_general(a, b, (((0,), (0,)), ((), ())), preferred_element_type=F32)


def block_ids(rows=BLK):
    p = lax.broadcasted_iota(jnp.int32, (EXP, rows, TOK), 0).reshape(EXP * rows, TOK)
    e = 4 * (p & 7) + (p >> 3)
    k = lax.broadcasted_iota(jnp.int32, (EXP, rows, TOK), 1).reshape(EXP * rows, TOK)
    return e, k


def slots_of(e, k):
    tens = jnp.where(k >= 30, 30, jnp.where(k >= 20, 20, jnp.where(k >= 10, 10, 0)))
    low = jnp.where(k < 35, e * CAP + k - tens, -1)
    high = jnp.where((k >= 30) & (k < 35), e * CAP + k - 30 + HALF, -1)
    return low, high


def pack_kernel(xt_ref, gt_ref, et_ref, out_ref, tgt_ref):
    yl = lax.axis_index("yl")
    e0 = et_ref[0:1, :]
    e1 = et_ref[1:2, :]
    xi = lax.broadcasted_iota(jnp.int32, (EXP, TOK), 0)
    named = ((xi == e0) | (xi == e1)).astype(F32).astype(BF)
    earlier = (
        lax.broadcasted_iota(jnp.int32, (TOK, TOK), 0) < lax.broadcasted_iota(jnp.int32, (TOK, TOK), 1)
    ).astype(F32).astype(BF)
    before = jnp.dot(named, earlier, preferred_element_type=F32)
    s0 = jnp.sum(jnp.where(xi == e0, before, 0.0), axis=0, keepdims=True).astype(jnp.int32)
    s1 = jnp.sum(jnp.where(xi == e1, before, 0.0), axis=0, keepdims=True).astype(jnp.int32)
    t0 = e0 * CAP + s0
    t1 = e1 * CAP + s1
    tgt_ref[0:1, :] = t0
    tgt_ref[1:2, :] = t1
    e, k = block_ids()
    low, high = slots_of(e, k)
    one = lambda hit: hit.astype(F32).astype(BF)
    m_low = jnp.concatenate([one(low == t0), one(low == t1)], axis=1)
    m_high = jnp.concatenate([one(high == t0), one(high == t1)], axis=1)

    def scaled(rows):
        x = rows.astype(F32)
        return jnp.concatenate([(x * gt_ref[0:1, :]).astype(BF), (x * gt_ref[1:2, :]).astype(BF)], axis=1)

    full = scaled(xt_ref[pl.ds(pl.multiple_of(64 * yl, 64), FULL), :])
    half = scaled(xt_ref[pl.ds(pl.multiple_of(FULL * (1 - yl), 64), 64), :])
    none = jnp.zeros_like(half)
    wide = nt(m_low, full)
    pair = nt(m_low, jnp.concatenate([half, none], axis=0)) + nt(m_high, jnp.concatenate([none, half], axis=0))
    picked = jnp.where(
        k < 10, wide[:, 0:128], jnp.where(k < 20, wide[:, 128:256], jnp.where(k < 30, wide[:, 256:384], pair))
    )
    out_ref[...] = picked.astype(BF)


def sort_kernel(in_ref, out_ref):
    n_in, rows = GRP * BLK, GRP * HALF
    q = lax.broadcasted_iota(jnp.int32, (rows, n_in), 0)
    col = lax.broadcasted_iota(jnp.int32, (rows, n_in), 1)
    gap = col - 35 * ((q * 205) >> 10) - q
    moves = jnp.concatenate([(gap == HALF * b).astype(F32).astype(BF) for b in range(7)], axis=0)
    both = jnp.concatenate([in_ref[0:n_in, :], in_ref[n_in : 2 * n_in, :]], axis=1)
    res = jnp.dot(moves, both, preferred_element_type=F32).astype(BF)
    for b in range(7):
        for g in range(2):
            block = res[b * rows : (b + 1) * rows, g * 128 : (g + 1) * 128]
            for t in range(TEN):
                at = t * PIECE + b * HROWS + g * rows
                out_ref[at : at + rows, :] = block


def stack_kernel(wd0, wd1, wg0, wg1, wu0, wu1, sg0, sg1, su0, su1, w_ref, sg_ref, su_ref, f_ref):
    step = pl.program_id(0)
    def stack(ref, first, blocks):
        for i, block in enumerate(blocks):
            at = first + i * FPAD
            ref[at + FPAD - 16 : at + FPAD, :] = jnp.zeros((16, ref.shape[1]), BF)
            ref[at : at + FF, :] = block[...]

    stack(w_ref, 0, (wd0, wd1, wg0, wg1, wu0, wu1))

    @pl.when(step == 0)
    def _():
        stack(sg_ref, 0, (sg0, sg1))
        stack(su_ref, 0, (su0, su1))
        core = lax.axis_index("core")
        r = lax.broadcasted_iota(jnp.int32, (ROWS, 2 * ROWS), 0)
        col = lax.broadcasted_iota(jnp.int32, (ROWS, 2 * ROWS), 1)
        h = (r >= HROWS).astype(jnp.int32)
        q = r - HROWS * h
        p = (q * 205) >> 10
        source = 4 * (p & 7) + (p >> 3)
        pick = (col == 2 * CAP * source + (q - HALF * p) + HALF * h + CAP * core).astype(F32).astype(BF)
        g = nt(pick, sg_ref[...])
        u = nt(pick, su_ref[...])
        sig = 1.0 / (1.0 + jnp.exp(-g))
        for i, factor in enumerate((u * sig * (1.0 + g * (1.0 - sig)), g * sig)):
            high = factor.astype(BF)
            f_ref[2 * i] = high
            f_ref[2 * i + 1] = (factor - high.astype(F32)).astype(BF)

    w_ref[6 * FPAD :, 0:FULL] = jnp.concatenate([f_ref[step], jnp.zeros((ROWS, FULL - 2 * FPAD), BF)], axis=1)


def main_kernel(in_ref, w_hbm, out_ref, r_ref, w_ref, f_ref, sems):
    down, rest = 2 * FPAD, 4 * FPAD
    pairs = [(w_hbm.at[pl.ds(0, down), :], w_ref.at[pl.ds(0, down), :])]
    for i in range(4):
        pairs.append((w_hbm.at[pl.ds(down + rest, ROWS), pl.ds(i * PAIR, FULL)], f_ref.at[i]))
    for i in range(4):
        at = (pl.ds(down, rest), pl.ds(i * PAIR, PAIR))
        pairs.append((w_hbm.at[at], w_ref.at[at]))
    copies = [pltpu.make_async_copy(src, dst, sems.at[i]) for i, (src, dst) in enumerate(pairs)]
    for copy in copies:
        copy.start()
    for i in range(4):
        base, even, odd = i * PAIR, i * PIECE, (4 + i) * PIECE
        for j in range(3):
            r_ref[:, base + 128 * j : base + 128 * (j + 1)] = in_ref[even + j * ROWS : even + (j + 1) * ROWS, :]
            at = base + 512 + 128 * j
            r_ref[:, at : at + 128] = in_ref[odd + j * ROWS : odd + (j + 1) * ROWS, :]
        eh = in_ref[even + 3 * ROWS : even + PIECE, :]
        oh = in_ref[odd + 3 * ROWS : odd + PIECE, :]
        r_ref[0:HROWS, base + FULL : base + 512] = jnp.concatenate([eh[:, :64], oh[:, :64]], axis=1)
        r_ref[HROWS:ROWS, base + FULL : base + 512] = jnp.concatenate([eh[:, 64:], oh[:, 64:]], axis=1)
    copies[0].wait()
    hidden = nt(r_ref[...], w_ref[0:down, :])
    for copy in copies[1:5]:
        copy.wait()
    part = lambda i: f_ref[i, :, 0:down].astype(F32)
    grads = jnp.concatenate([hidden * (part(0) + part(1)), hidden * (part(2) + part(3))], axis=1).astype(BF)
    for i in range(4):
        base, even, odd = i * PAIR, 2 * i * PIECE, (2 * i + 1) * PIECE
        copies[5 + i].wait()
        acc = jnp.dot(grads, w_ref[down:, base : base + PAIR], preferred_element_type=F32).astype(BF)
        for j in range(3):
            out_ref[even + j * ROWS : even + (j + 1) * ROWS, :] = acc[:, 128 * j : 128 * (j + 1)]
            out_ref[odd + j * ROWS : odd + (j + 1) * ROWS, :] = acc[:, 512 + 128 * j : 512 + 128 * (j + 1)]
        lo = acc[0:HROWS, FULL:512]
        hi = acc[HROWS:ROWS, FULL:512]
        out_ref[even + 3 * ROWS : even + PIECE, :] = jnp.concatenate([lo[:, :64], hi[:, :64]], axis=1)
        out_ref[odd + 3 * ROWS : odd + PIECE, :] = jnp.concatenate([lo[:, 64:], hi[:, 64:]], axis=1)


def unsort_kernel(in_ref, out_ref):
    rows = GRP * HALF
    n_out = GRP * BLK
    q = lax.broadcasted_iota(jnp.int32, (n_out, rows), 1)
    row = lax.broadcasted_iota(jnp.int32, (n_out, rows), 0)
    gap = row - 35 * ((q * 205) >> 10) - q
    res = [None, None]
    for b in range(7):
        move = (gap == HALF * b).astype(F32).astype(BF)
        cols = []
        for g in range(2):
            total = None
            for t in range(TEN):
                at = t * PIECE + b * HROWS + g * rows
                part = in_ref[at : at + rows, :].astype(F32)
                total = part if total is None else total + part
            cols.append(total.astype(BF))
        term = jnp.dot(move, jnp.concatenate(cols, axis=1), preferred_element_type=F32)
        for g in range(2):
            t = term[:, g * 128 : (g + 1) * 128]
            res[g] = t if res[g] is None else res[g] + t
    for g in range(2):
        out_ref[g * n_out : (g + 1) * n_out, :] = res[g].astype(BF)


def combine_kernel(in_ref, tgt_ref, out_ref):
    yl = lax.axis_index("yl")
    t0 = tgt_ref[0:1, :]
    t1 = tgt_ref[1:2, :]
    e, k = block_ids()
    low, high = slots_of(e, k)
    hit = ((low == t0) | (low == t1)).astype(F32)
    cut = lambda a, b: jnp.where((k >= a) & (k < b), hit, 0.0).astype(BF)
    hit_high = ((high == t0) | (high == t1)).astype(F32).astype(BF)
    take = jnp.concatenate([cut(0, 10), cut(10, 20), cut(20, 30), cut(30, 35), hit_high], axis=1)
    res = tn(in_ref[...], take)
    start = pl.multiple_of(64 * yl, 64)
    for j in range(3):
        out_ref[pl.ds(pl.multiple_of(start + 128 * j, 64), 128), :] = res[:, 128 * j : 128 * (j + 1)].astype(BF)
    half = res[0:64, FULL:512] + res[64:128, 512:640]
    out_ref[pl.ds(pl.multiple_of(FULL * (1 - yl), 64), 64), :] = half.astype(BF)


def call(kernel, outs, specs, flops, moved, scratch=(), limit=SMALL, grid=(), out_specs=VM):
    if isinstance(outs, list) and not isinstance(out_specs, list):
        out_specs = [out_specs] * len(outs)
    return pl.pallas_call(
        kernel,
        out_shape=outs,
        grid=grid,
        in_specs=specs,
        out_specs=out_specs,
        scratch_shapes=list(scratch),
        cost_estimate=pl.CostEstimate(flops=flops, bytes_accessed=moved, transcendentals=0),
        compiler_params=pltpu.CompilerParams(vmem_limit_bytes=limit),
    )


def sds(shape, dtype=BF):
    return jax.ShapeDtypeStruct(shape, dtype)


def swap_core(a):
    return lax.ppermute(a, "core", [(0, 1), (1, 0)])


def exchange(a, axes, n):
    blocks = a.reshape(n, a.shape[0] // n, a.shape[1])
    return lax.all_to_all(blocks, axes, split_axis=0, concat_axis=0, tiled=True).reshape(a.shape)


def shards(out_grad, gate_probs, expert_ids, saved_gate, saved_up, w_gate, w_up, w_down):
    packed, target = call(
        pack_kernel,
        [sds((EXP * BLK, 128)), sds((2, TOK), jnp.int32)],
        [VM, VM, VM],
        10**9,
        10**6,
        limit=BIG,
    )(out_grad.T, gate_probs.T, expert_ids.T)
    got = exchange(packed, ("yh", "z"), EXP)
    spread = call(sort_kernel, sds((TEN * PIECE, 128)), [VM], 10**9, 3 * 10**6)(got)
    pieces = exchange(spread, ("yl", "x"), TEN)

    operands = []
    for a in (w_down, w_gate, w_up, saved_gate, saved_up):
        operands += [a, swap_core(a)]
    block = pl.BlockSpec((FF, PAIR), lambda i: (0, i))
    saved = pl.BlockSpec((FF, 2 * ROWS), lambda i: (0, 0))
    weights = call(
        stack_kernel,
        sds((6 * FPAD + ROWS, D)),
        [block] * 6 + [saved] * 4,
        5 * 10**8,
        16 * 10**6,
        scratch=[pltpu.VMEM((2 * FPAD, 2 * ROWS), BF)] * 2 + [pltpu.VMEM((4, ROWS, 2 * FPAD), BF)],
        limit=BIG,
        grid=(4,),
        out_specs=pl.BlockSpec((6 * FPAD + ROWS, PAIR), lambda i: (0, i)),
    )(*operands)
    parts = call(
        main_kernel,
        sds((TEN * PIECE, 128)),
        [VM, AN],
        23 * 10**8,
        12 * 10**6,
        scratch=[
            pltpu.VMEM((ROWS, D), BF),
            pltpu.VMEM((6 * FPAD, D), BF),
            pltpu.VMEM((4, ROWS, FULL), BF),
            pltpu.SemaphoreType.DMA((9,)),
        ],
        limit=MID,
    )(pieces, weights)
    home = exchange(parts, ("x", "yl"), TEN)
    summed = call(unsort_kernel, sds((EXP * BLK, 128)), [VM], 10**9, 3 * 10**6)(home)
    back = exchange(summed, ("yh", "z"), EXP)
    out_t = call(combine_kernel, sds((FEAT, TOK)), [VM, VM], 10**9, 10**6)(back, target)
    return out_t.T


def solution(mesh):
    grid = Mesh(mesh.devices.reshape(8, 4, 2, 4, 2), ("z", "yh", "core", "x", "yl"))
    ex, te = ("z", "yh", "core"), ("x", "yl")
    return jax.shard_map(
        shards,
        mesh=grid,
        in_specs=(P(ex, te), P(ex, None), P(ex, None)) + (P(ex + te, None),) * 5,
        out_specs=P(ex, te),
        check_vma=False,
    )
```

```python
import jax
import jax.numpy as jnp
from jax import lax
from jax.experimental import pallas as pl
from jax.experimental.pallas import tpu as pltpu
from jax.sharding import Mesh, PartitionSpec as P

CAP = 10
HALF = CAP // 2
BLK = 40
EXP = 32
TEN = 8
BIG = 62 * 10**6
MID = 50 * 10**6
SMALL = 16 * 10**6
TOK = 128
FEAT = 448
FULL = 384
FF = 152
PAIR = 2 * FEAT
ROWS = EXP * CAP
HROWS = ROWS // 2
PIECE = 7 * HROWS
GRP = EXP // 2
FPAD = 160
D = 3584

BF = jnp.bfloat16
F32 = jnp.float32
VM = pl.BlockSpec(memory_space=pltpu.VMEM)
AN = pl.BlockSpec(memory_space=pl.ANY)


def nt(a, b):
    return lax.dot_general(a, b, (((1,), (1,)), ((), ())), preferred_element_type=F32)


def tn(a, b):
    return lax.dot_general(a, b, (((0,), (0,)), ((), ())), preferred_element_type=F32)


def block_ids(rows=BLK):
    e = lax.broadcasted_iota(jnp.int32, (EXP, rows, TOK), 0).reshape(EXP * rows, TOK)
    k = lax.broadcasted_iota(jnp.int32, (EXP, rows, TOK), 1).reshape(EXP * rows, TOK)
    return e, k


def slots_of(e, k):
    tens = jnp.where(k >= 30, 30, jnp.where(k >= 20, 20, jnp.where(k >= 10, 10, 0)))
    low = jnp.where(k < 35, e * CAP + k - tens, -1)
    high = jnp.where((k >= 30) & (k < 35), e * CAP + k - 30 + HALF, -1)
    return low, high


def pack_kernel(xt_ref, gt_ref, et_ref, out_ref, tgt_ref):
    yl = lax.axis_index("yl")
    e0 = et_ref[0:1, :]
    e1 = et_ref[1:2, :]
    xi = lax.broadcasted_iota(jnp.int32, (EXP, TOK), 0)
    named = ((xi == e0) | (xi == e1)).astype(F32).astype(BF)
    earlier = (
        lax.broadcasted_iota(jnp.int32, (TOK, TOK), 0) < lax.broadcasted_iota(jnp.int32, (TOK, TOK), 1)
    ).astype(F32).astype(BF)
    before = jnp.dot(named, earlier, preferred_element_type=F32)
    s0 = jnp.sum(jnp.where(xi == e0, before, 0.0), axis=0, keepdims=True).astype(jnp.int32)
    s1 = jnp.sum(jnp.where(xi == e1, before, 0.0), axis=0, keepdims=True).astype(jnp.int32)
    t0 = e0 * CAP + s0
    t1 = e1 * CAP + s1
    tgt_ref[0:1, :] = t0
    tgt_ref[1:2, :] = t1
    e, k = block_ids()
    low, high = slots_of(e, k)
    one = lambda hit: hit.astype(F32).astype(BF)
    m_low = jnp.concatenate([one(low == t0), one(low == t1)], axis=1)
    m_high = jnp.concatenate([one(high == t0), one(high == t1)], axis=1)

    def scaled(rows):
        x = rows.astype(F32)
        return jnp.concatenate([(x * gt_ref[0:1, :]).astype(BF), (x * gt_ref[1:2, :]).astype(BF)], axis=1)

    full = scaled(xt_ref[pl.ds(pl.multiple_of(64 * yl, 64), FULL), :])
    half = scaled(xt_ref[pl.ds(pl.multiple_of(FULL * (1 - yl), 64), 64), :])
    none = jnp.zeros_like(half)
    wide = nt(m_low, full)
    pair = nt(m_low, jnp.concatenate([half, none], axis=0)) + nt(m_high, jnp.concatenate([none, half], axis=0))
    picked = jnp.where(
        k < 10, wide[:, 0:128], jnp.where(k < 20, wide[:, 128:256], jnp.where(k < 30, wide[:, 256:384], pair))
    )
    out_ref[...] = picked.astype(BF)


def sort_kernel(in_ref, out_ref):
    n_in, rows = GRP * BLK, GRP * HALF
    q = lax.broadcasted_iota(jnp.int32, (rows, n_in), 0)
    col = lax.broadcasted_iota(jnp.int32, (rows, n_in), 1)
    gap = col - 35 * ((q * 205) >> 10) - q
    moves = jnp.concatenate([(gap == HALF * b).astype(F32).astype(BF) for b in range(7)], axis=0)
    both = jnp.concatenate([in_ref[0:n_in, :], in_ref[n_in : 2 * n_in, :]], axis=1)
    res = jnp.dot(moves, both, preferred_element_type=F32).astype(BF)
    for b in range(7):
        for g in range(2):
            block = res[b * rows : (b + 1) * rows, g * 128 : (g + 1) * 128]
            for t in range(TEN):
                at = t * PIECE + b * HROWS + g * rows
                out_ref[at : at + rows, :] = block


def stack_kernel(wd0, wd1, wg0, wg1, wu0, wu1, sg0, sg1, su0, su1, w_ref, sg_ref, su_ref, f_ref):
    step = pl.program_id(0)
    def stack(ref, first, blocks):
        for i, block in enumerate(blocks):
            at = first + i * FPAD
            ref[at + FPAD - 16 : at + FPAD, :] = jnp.zeros((16, ref.shape[1]), BF)
            ref[at : at + FF, :] = block[...]

    stack(w_ref, 0, (wd0, wd1, wg0, wg1, wu0, wu1))

    @pl.when(step == 0)
    def _():
        stack(sg_ref, 0, (sg0, sg1))
        stack(su_ref, 0, (su0, su1))
        core = lax.axis_index("core")
        r = lax.broadcasted_iota(jnp.int32, (ROWS, 2 * ROWS), 0)
        col = lax.broadcasted_iota(jnp.int32, (ROWS, 2 * ROWS), 1)
        h = (r >= HROWS).astype(jnp.int32)
        q = r - HROWS * h
        pick = (col == 15 * ((q * 205) >> 10) + q + HALF * h + CAP * core).astype(F32).astype(BF)
        g = nt(pick, sg_ref[...])
        u = nt(pick, su_ref[...])
        sig = 1.0 / (1.0 + jnp.exp(-g))
        for i, factor in enumerate((u * sig * (1.0 + g * (1.0 - sig)), g * sig)):
            high = factor.astype(BF)
            f_ref[2 * i] = high
            f_ref[2 * i + 1] = (factor - high.astype(F32)).astype(BF)

    w_ref[6 * FPAD :, 0:FULL] = jnp.concatenate([f_ref[step], jnp.zeros((ROWS, FULL - 2 * FPAD), BF)], axis=1)


def main_kernel(in_ref, w_hbm, out_ref, r_ref, w_ref, f_ref, sems):
    down, rest = 2 * FPAD, 4 * FPAD
    pairs = []
    for i in range(4):
        at = (pl.ds(0, down), pl.ds(i * PAIR, PAIR))
        pairs.append((w_hbm.at[at], w_ref.at[at]))
    for i in range(4):
        pairs.append((w_hbm.at[pl.ds(down + rest, ROWS), pl.ds(i * PAIR, FULL)], f_ref.at[i]))
    for i in range(4):
        at = (pl.ds(down, rest), pl.ds(i * PAIR, PAIR))
        pairs.append((w_hbm.at[at], w_ref.at[at]))
    copies = [pltpu.make_async_copy(src, dst, sems.at[i]) for i, (src, dst) in enumerate(pairs)]
    for copy in copies:
        copy.start()
    hidden = None
    for i in range(4):
        base, even, odd = i * PAIR, i * PIECE, (4 + i) * PIECE
        for j in range(3):
            r_ref[:, base + 128 * j : base + 128 * (j + 1)] = in_ref[even + j * ROWS : even + (j + 1) * ROWS, :]
            at = base + 512 + 128 * j
            r_ref[:, at : at + 128] = in_ref[odd + j * ROWS : odd + (j + 1) * ROWS, :]
        eh = in_ref[even + 3 * ROWS : even + PIECE, :]
        oh = in_ref[odd + 3 * ROWS : odd + PIECE, :]
        r_ref[0:HROWS, base + FULL : base + 512] = jnp.concatenate([eh[:, :64], oh[:, :64]], axis=1)
        r_ref[HROWS:ROWS, base + FULL : base + 512] = jnp.concatenate([eh[:, 64:], oh[:, 64:]], axis=1)
        copies[i].wait()
        term = nt(r_ref[:, base : base + PAIR], w_ref[0:down, base : base + PAIR])
        hidden = term if hidden is None else hidden + term
    for copy in copies[4:8]:
        copy.wait()
    part = lambda i: f_ref[i, :, 0:down].astype(F32)
    grads = jnp.concatenate([hidden * (part(0) + part(1)), hidden * (part(2) + part(3))], axis=1).astype(BF)
    for i in range(4):
        base, even, odd = i * PAIR, 2 * i * PIECE, (2 * i + 1) * PIECE
        copies[8 + i].wait()
        acc = jnp.dot(grads, w_ref[down:, base : base + PAIR], preferred_element_type=F32).astype(BF)
        for j in range(3):
            out_ref[even + j * ROWS : even + (j + 1) * ROWS, :] = acc[:, 128 * j : 128 * (j + 1)]
            out_ref[odd + j * ROWS : odd + (j + 1) * ROWS, :] = acc[:, 512 + 128 * j : 512 + 128 * (j + 1)]
        lo = acc[0:HROWS, FULL:512]
        hi = acc[HROWS:ROWS, FULL:512]
        out_ref[even + 3 * ROWS : even + PIECE, :] = jnp.concatenate([lo[:, :64], hi[:, :64]], axis=1)
        out_ref[odd + 3 * ROWS : odd + PIECE, :] = jnp.concatenate([lo[:, 64:], hi[:, 64:]], axis=1)


def unsort_kernel(in_ref, out_ref):
    rows = GRP * HALF
    n_out = GRP * BLK
    q = lax.broadcasted_iota(jnp.int32, (n_out, rows), 1)
    row = lax.broadcasted_iota(jnp.int32, (n_out, rows), 0)
    gap = row - 35 * ((q * 205) >> 10) - q
    res = [None, None]
    for b in range(7):
        move = (gap == HALF * b).astype(F32).astype(BF)
        cols = []
        for g in range(2):
            total = None
            for t in range(TEN):
                at = t * PIECE + b * HROWS + g * rows
                part = in_ref[at : at + rows, :].astype(F32)
                total = part if total is None else total + part
            cols.append(total.astype(BF))
        term = jnp.dot(move, jnp.concatenate(cols, axis=1), preferred_element_type=F32)
        for g in range(2):
            t = term[:, g * 128 : (g + 1) * 128]
            res[g] = t if res[g] is None else res[g] + t
    for g in range(2):
        out_ref[g * n_out : (g + 1) * n_out, :] = res[g].astype(BF)


def combine_kernel(in_ref, tgt_ref, out_ref):
    yl = lax.axis_index("yl")
    t0 = tgt_ref[0:1, :]
    t1 = tgt_ref[1:2, :]
    e, k = block_ids()
    low, high = slots_of(e, k)
    hit = ((low == t0) | (low == t1)).astype(F32)
    cut = lambda a, b: jnp.where((k >= a) & (k < b), hit, 0.0).astype(BF)
    hit_high = ((high == t0) | (high == t1)).astype(F32).astype(BF)
    take = jnp.concatenate([cut(0, 10), cut(10, 20), cut(20, 30), cut(30, 35), hit_high], axis=1)
    res = tn(in_ref[...], take)
    start = pl.multiple_of(64 * yl, 64)
    for j in range(3):
        out_ref[pl.ds(pl.multiple_of(start + 128 * j, 64), 128), :] = res[:, 128 * j : 128 * (j + 1)].astype(BF)
    half = res[0:64, FULL:512] + res[64:128, 512:640]
    out_ref[pl.ds(pl.multiple_of(FULL * (1 - yl), 64), 64), :] = half.astype(BF)


def call(kernel, outs, specs, flops, moved, scratch=(), limit=SMALL, grid=(), out_specs=VM):
    if isinstance(outs, list) and not isinstance(out_specs, list):
        out_specs = [out_specs] * len(outs)
    return pl.pallas_call(
        kernel,
        out_shape=outs,
        grid=grid,
        in_specs=specs,
        out_specs=out_specs,
        scratch_shapes=list(scratch),
        cost_estimate=pl.CostEstimate(flops=flops, bytes_accessed=moved, transcendentals=0),
        compiler_params=pltpu.CompilerParams(vmem_limit_bytes=limit),
    )


def sds(shape, dtype=BF):
    return jax.ShapeDtypeStruct(shape, dtype)


def swap_core(a):
    return lax.ppermute(a, "core", [(0, 1), (1, 0)])


def exchange(a, axes, n):
    blocks = a.reshape(n, a.shape[0] // n, a.shape[1])
    return lax.all_to_all(blocks, axes, split_axis=0, concat_axis=0, tiled=True).reshape(a.shape)


def shards(out_grad, gate_probs, expert_ids, saved_gate, saved_up, w_gate, w_up, w_down):
    packed, target = call(
        pack_kernel,
        [sds((EXP * BLK, 128)), sds((2, TOK), jnp.int32)],
        [VM, VM, VM],
        10**9,
        10**6,
        limit=BIG,
    )(out_grad.T, gate_probs.T, expert_ids.T)
    got = exchange(packed, ("z", "yh"), EXP)
    spread = call(sort_kernel, sds((TEN * PIECE, 128)), [VM], 10**9, 3 * 10**6)(got)
    pieces = exchange(spread, ("yl", "x"), TEN)

    operands = []
    for a in (w_down, w_gate, w_up, saved_gate, saved_up):
        operands += [a, swap_core(a)]
    block = pl.BlockSpec((FF, PAIR), lambda i: (0, i))
    saved = pl.BlockSpec((FF, 2 * ROWS), lambda i: (0, 0))
    weights = call(
        stack_kernel,
        sds((6 * FPAD + ROWS, D)),
        [block] * 6 + [saved] * 4,
        5 * 10**8,
        16 * 10**6,
        scratch=[pltpu.VMEM((2 * FPAD, 2 * ROWS), BF)] * 2 + [pltpu.VMEM((4, ROWS, 2 * FPAD), BF)],
        limit=BIG,
        grid=(4,),
        out_specs=pl.BlockSpec((6 * FPAD + ROWS, PAIR), lambda i: (0, i)),
    )(*operands)
    parts = call(
        main_kernel,
        sds((TEN * PIECE, 128)),
        [VM, AN],
        23 * 10**8,
        12 * 10**6,
        scratch=[
            pltpu.VMEM((ROWS, D), BF),
            pltpu.VMEM((6 * FPAD, D), BF),
            pltpu.VMEM((4, ROWS, FULL), BF),
            pltpu.SemaphoreType.DMA((12,)),
        ],
        limit=MID,
    )(pieces, weights)
    home = exchange(parts, ("x", "yl"), TEN)
    summed = call(unsort_kernel, sds((EXP * BLK, 128)), [VM], 10**9, 3 * 10**6)(home)
    back = exchange(summed, ("z", "yh"), EXP)
    out_t = call(combine_kernel, sds((FEAT, TOK)), [VM, VM], 10**9, 10**6)(back, target)
    return out_t.T


def solution(mesh):
    grid = Mesh(mesh.devices.reshape(8, 4, 2, 4, 2), ("z", "yh", "core", "x", "yl"))
    ex, te = ("z", "yh", "core"), ("x", "yl")
    return jax.shard_map(
        shards,
        mesh=grid,
        in_specs=(P(ex, te), P(ex, None), P(ex, None)) + (P(ex + te, None),) * 5,
        out_specs=P(ex, te),
        check_vma=False,
    )
```

```python
import jax
import jax.numpy as jnp
from jax import lax
from jax.experimental import pallas as pl
from jax.experimental.pallas import tpu as pltpu
from jax.sharding import Mesh, PartitionSpec as P

CAP = 10
HALF = CAP // 2
BLK = 40
EXP = 32
TEN = 8
BIG = 62 * 10**6
MID = 50 * 10**6
SMALL = 16 * 10**6
TOK = 128
FEAT = 448
FULL = 384
FF = 152
PAIR = 2 * FEAT
ROWS = EXP * CAP
HROWS = ROWS // 2
PIECE = 7 * HROWS
GRP = EXP // 2
FPAD = 160
D = 3584

BF = jnp.bfloat16
F32 = jnp.float32
VM = pl.BlockSpec(memory_space=pltpu.VMEM)
AN = pl.BlockSpec(memory_space=pl.ANY)


def nt(a, b):
    return lax.dot_general(a, b, (((1,), (1,)), ((), ())), preferred_element_type=F32)


def tn(a, b):
    return lax.dot_general(a, b, (((0,), (0,)), ((), ())), preferred_element_type=F32)


def block_ids(rows=BLK):
    e = lax.broadcasted_iota(jnp.int32, (EXP, rows, TOK), 0).reshape(EXP * rows, TOK)
    k = lax.broadcasted_iota(jnp.int32, (EXP, rows, TOK), 1).reshape(EXP * rows, TOK)
    return e, k


def slots_of(e, k):
    tens = jnp.where(k >= 30, 30, jnp.where(k >= 20, 20, jnp.where(k >= 10, 10, 0)))
    low = jnp.where(k < 35, e * CAP + k - tens, -1)
    high = jnp.where((k >= 30) & (k < 35), e * CAP + k - 30 + HALF, -1)
    return low, high


def pack_kernel(xt_ref, gt_ref, et_ref, out_ref, tgt_ref):
    yl = lax.axis_index("yl")
    e0 = et_ref[0:1, :]
    e1 = et_ref[1:2, :]
    xi = lax.broadcasted_iota(jnp.int32, (EXP, TOK), 0)
    named = ((xi == e0) | (xi == e1)).astype(F32).astype(BF)
    earlier = (
        lax.broadcasted_iota(jnp.int32, (TOK, TOK), 0) < lax.broadcasted_iota(jnp.int32, (TOK, TOK), 1)
    ).astype(F32).astype(BF)
    before = jnp.dot(named, earlier, preferred_element_type=F32)
    s0 = jnp.sum(jnp.where(xi == e0, before, 0.0), axis=0, keepdims=True).astype(jnp.int32)
    s1 = jnp.sum(jnp.where(xi == e1, before, 0.0), axis=0, keepdims=True).astype(jnp.int32)
    t0 = e0 * CAP + s0
    t1 = e1 * CAP + s1
    tgt_ref[0:1, :] = t0
    tgt_ref[1:2, :] = t1
    e, k = block_ids()
    low, high = slots_of(e, k)
    one = lambda hit: hit.astype(F32).astype(BF)
    m_low = jnp.concatenate([one(low == t0), one(low == t1)], axis=1)
    m_high = jnp.concatenate([one(high == t0), one(high == t1)], axis=1)

    def scaled(rows):
        x = rows.astype(F32)
        return jnp.concatenate([(x * gt_ref[0:1, :]).astype(BF), (x * gt_ref[1:2, :]).astype(BF)], axis=1)

    full = scaled(xt_ref[pl.ds(pl.multiple_of(64 * yl, 64), FULL), :])
    half = scaled(xt_ref[pl.ds(pl.multiple_of(FULL * (1 - yl), 64), 64), :])
    none = jnp.zeros_like(half)
    wide = nt(m_low, full)
    pair = nt(m_low, jnp.concatenate([half, none], axis=0)) + nt(m_high, jnp.concatenate([none, half], axis=0))
    picked = jnp.where(
        k < 10, wide[:, 0:128], jnp.where(k < 20, wide[:, 128:256], jnp.where(k < 30, wide[:, 256:384], pair))
    )
    out_ref[...] = picked.astype(BF)


def sort_kernel(in_ref, out_ref):
    n_in, rows = GRP * BLK, GRP * HALF
    q = lax.broadcasted_iota(jnp.int32, (rows, n_in), 0)
    col = lax.broadcasted_iota(jnp.int32, (rows, n_in), 1)
    gap = col - 35 * ((q * 205) >> 10) - q
    moves = jnp.concatenate([(gap == HALF * b).astype(F32).astype(BF) for b in range(7)], axis=0)
    both = jnp.concatenate([in_ref[0:n_in, :], in_ref[n_in : 2 * n_in, :]], axis=1)
    res = jnp.dot(moves, both, preferred_element_type=F32).astype(BF)
    for b in range(7):
        for g in range(2):
            block = res[b * rows : (b + 1) * rows, g * 128 : (g + 1) * 128]
            for t in range(TEN):
                at = t * PIECE + b * HROWS + g * rows
                out_ref[at : at + rows, :] = block


def stack_kernel(wd0, wd1, wg0, wg1, wu0, wu1, sg0, sg1, su0, su1, w_ref, sg_ref, su_ref, f_ref):
    step = pl.program_id(0)
    def stack(ref, first, blocks):
        for i, block in enumerate(blocks):
            at = first + i * FPAD
            ref[at + FPAD - 16 : at + FPAD, :] = jnp.zeros((16, ref.shape[1]), BF)
            ref[at : at + FF, :] = block[...]

    stack(w_ref, 0, (wd0, wd1, wg0, wg1, wu0, wu1))

    @pl.when(step == 0)
    def _():
        stack(sg_ref, 0, (sg0, sg1))
        stack(su_ref, 0, (su0, su1))
        core = lax.axis_index("core")
        r = lax.broadcasted_iota(jnp.int32, (ROWS, 2 * ROWS), 0)
        col = lax.broadcasted_iota(jnp.int32, (ROWS, 2 * ROWS), 1)
        h = (r >= HROWS).astype(jnp.int32)
        q = r - HROWS * h
        pick = (col == 15 * ((q * 205) >> 10) + q + HALF * h + CAP * core).astype(F32).astype(BF)
        g = nt(pick, sg_ref[...])
        u = nt(pick, su_ref[...])
        sig = 1.0 / (1.0 + jnp.exp(-g))
        for i, factor in enumerate((u * sig * (1.0 + g * (1.0 - sig)), g * sig)):
            high = factor.astype(BF)
            f_ref[2 * i] = high
            f_ref[2 * i + 1] = (factor - high.astype(F32)).astype(BF)

    w_ref[6 * FPAD :, 0:FULL] = jnp.concatenate([f_ref[step], jnp.zeros((ROWS, FULL - 2 * FPAD), BF)], axis=1)


def main_kernel(in_ref, w_hbm, out_ref, r_ref, w_ref, f_ref, sems):
    down, rest = 2 * FPAD, 4 * FPAD
    pairs = [(w_hbm.at[pl.ds(0, down), :], w_ref.at[pl.ds(0, down), :])]
    for i in range(4):
        pairs.append((w_hbm.at[pl.ds(down + rest, ROWS), pl.ds(i * PAIR, FULL)], f_ref.at[i]))
    for i in range(4):
        at = (pl.ds(down, rest), pl.ds(i * PAIR, PAIR))
        pairs.append((w_hbm.at[at], w_ref.at[at]))
    copies = [pltpu.make_async_copy(src, dst, sems.at[i]) for i, (src, dst) in enumerate(pairs)]
    for copy in copies:
        copy.start()
    for i in range(4):
        base, even, odd = i * PAIR, 2 * i * PIECE, (2 * i + 1) * PIECE
        for j in range(3):
            r_ref[:, base + 128 * j : base + 128 * (j + 1)] = in_ref[even + j * ROWS : even + (j + 1) * ROWS, :]
            at = base + 512 + 128 * j
            r_ref[:, at : at + 128] = in_ref[odd + j * ROWS : odd + (j + 1) * ROWS, :]
        eh = in_ref[even + 3 * ROWS : even + PIECE, :]
        oh = in_ref[odd + 3 * ROWS : odd + PIECE, :]
        r_ref[0:HROWS, base + FULL : base + 512] = jnp.concatenate([eh[:, :64], oh[:, :64]], axis=1)
        r_ref[HROWS:ROWS, base + FULL : base + 512] = jnp.concatenate([eh[:, 64:], oh[:, 64:]], axis=1)
    copies[0].wait()
    hidden = nt(r_ref[...], w_ref[0:down, :])
    for copy in copies[1:5]:
        copy.wait()
    part = lambda i: f_ref[i, :, 0:down].astype(F32)
    grads = jnp.concatenate([hidden * (part(0) + part(1)), hidden * (part(2) + part(3))], axis=1).astype(BF)
    for i in range(4):
        base, even, odd = i * PAIR, 2 * i * PIECE, (2 * i + 1) * PIECE
        copies[5 + i].wait()
        acc = jnp.dot(grads, w_ref[down:, base : base + PAIR], preferred_element_type=F32).astype(BF)
        for j in range(3):
            out_ref[even + j * ROWS : even + (j + 1) * ROWS, :] = acc[:, 128 * j : 128 * (j + 1)]
            out_ref[odd + j * ROWS : odd + (j + 1) * ROWS, :] = acc[:, 512 + 128 * j : 512 + 128 * (j + 1)]
        lo = acc[0:HROWS, FULL:512]
        hi = acc[HROWS:ROWS, FULL:512]
        out_ref[even + 3 * ROWS : even + PIECE, :] = jnp.concatenate([lo[:, :64], hi[:, :64]], axis=1)
        out_ref[odd + 3 * ROWS : odd + PIECE, :] = jnp.concatenate([lo[:, 64:], hi[:, 64:]], axis=1)


def unsort_kernel(in_ref, out_ref):
    rows = GRP * HALF
    n_out = GRP * BLK
    q = lax.broadcasted_iota(jnp.int32, (n_out, rows), 1)
    row = lax.broadcasted_iota(jnp.int32, (n_out, rows), 0)
    gap = row - 35 * ((q * 205) >> 10) - q
    res = [None, None]
    for b in range(7):
        move = (gap == HALF * b).astype(F32).astype(BF)
        cols = []
        for g in range(2):
            total = None
            for t in range(TEN):
                at = t * PIECE + b * HROWS + g * rows
                part = in_ref[at : at + rows, :].astype(F32)
                total = part if total is None else total + part
            cols.append(total.astype(BF))
        term = jnp.dot(move, jnp.concatenate(cols, axis=1), preferred_element_type=F32)
        for g in range(2):
            t = term[:, g * 128 : (g + 1) * 128]
            res[g] = t if res[g] is None else res[g] + t
    for g in range(2):
        out_ref[g * n_out : (g + 1) * n_out, :] = res[g].astype(BF)


def combine_kernel(in_ref, tgt_ref, out_ref):
    yl = lax.axis_index("yl")
    t0 = tgt_ref[0:1, :]
    t1 = tgt_ref[1:2, :]
    e, k = block_ids()
    low, high = slots_of(e, k)
    hit = ((low == t0) | (low == t1)).astype(F32)
    cut = lambda a, b: jnp.where((k >= a) & (k < b), hit, 0.0).astype(BF)
    hit_high = ((high == t0) | (high == t1)).astype(F32).astype(BF)
    take = jnp.concatenate([cut(0, 10), cut(10, 20), cut(20, 30), cut(30, 35), hit_high], axis=1)
    res = tn(in_ref[...], take)
    start = pl.multiple_of(64 * yl, 64)
    for j in range(3):
        out_ref[pl.ds(pl.multiple_of(start + 128 * j, 64), 128), :] = res[:, 128 * j : 128 * (j + 1)].astype(BF)
    half = res[0:64, FULL:512] + res[64:128, 512:640]
    out_ref[pl.ds(pl.multiple_of(FULL * (1 - yl), 64), 64), :] = half.astype(BF)


def call(kernel, outs, specs, flops, moved, scratch=(), limit=SMALL, grid=(), out_specs=VM):
    if isinstance(outs, list) and not isinstance(out_specs, list):
        out_specs = [out_specs] * len(outs)
    return pl.pallas_call(
        kernel,
        out_shape=outs,
        grid=grid,
        in_specs=specs,
        out_specs=out_specs,
        scratch_shapes=list(scratch),
        cost_estimate=pl.CostEstimate(flops=flops, bytes_accessed=moved, transcendentals=0),
        compiler_params=pltpu.CompilerParams(vmem_limit_bytes=limit),
    )


def sds(shape, dtype=BF):
    return jax.ShapeDtypeStruct(shape, dtype)


def swap_core(a):
    return lax.ppermute(a, "core", [(0, 1), (1, 0)])


def exchange(a, axes, n):
    blocks = a.reshape(n, a.shape[0] // n, a.shape[1])
    return lax.all_to_all(blocks, axes, split_axis=0, concat_axis=0, tiled=True).reshape(a.shape)


def shards(out_grad, gate_probs, expert_ids, saved_gate, saved_up, w_gate, w_up, w_down):
    packed, target = call(
        pack_kernel,
        [sds((EXP * BLK, 128)), sds((2, TOK), jnp.int32)],
        [VM, VM, VM],
        10**9,
        10**6,
        limit=BIG,
    )(out_grad.T, gate_probs.T, expert_ids.T)
    got = exchange(packed, ("z", "yh"), EXP)
    spread = call(sort_kernel, sds((TEN * PIECE, 128)), [VM], 10**9, 3 * 10**6)(got)
    pieces = exchange(spread, ("x", "yl"), TEN)

    operands = []
    for a in (w_down, w_gate, w_up, saved_gate, saved_up):
        operands += [a, swap_core(a)]
    block = pl.BlockSpec((FF, PAIR), lambda i: (0, i))
    saved = pl.BlockSpec((FF, 2 * ROWS), lambda i: (0, 0))
    weights = call(
        stack_kernel,
        sds((6 * FPAD + ROWS, D)),
        [block] * 6 + [saved] * 4,
        5 * 10**8,
        16 * 10**6,
        scratch=[pltpu.VMEM((2 * FPAD, 2 * ROWS), BF)] * 2 + [pltpu.VMEM((4, ROWS, 2 * FPAD), BF)],
        limit=BIG,
        grid=(4,),
        out_specs=pl.BlockSpec((6 * FPAD + ROWS, PAIR), lambda i: (0, i)),
    )(*operands)
    parts = call(
        main_kernel,
        sds((TEN * PIECE, 128)),
        [VM, AN],
        23 * 10**8,
        12 * 10**6,
        scratch=[
            pltpu.VMEM((ROWS, D), BF),
            pltpu.VMEM((6 * FPAD, D), BF),
            pltpu.VMEM((4, ROWS, FULL), BF),
            pltpu.SemaphoreType.DMA((9,)),
        ],
        limit=MID,
    )(pieces, weights)
    home = exchange(parts, ("x", "yl"), TEN)
    summed = call(unsort_kernel, sds((EXP * BLK, 128)), [VM], 10**9, 3 * 10**6)(home)
    back = exchange(summed, ("z", "yh"), EXP)
    out_t = call(combine_kernel, sds((FEAT, TOK)), [VM, VM], 10**9, 10**6)(back, target)
    return out_t.T


def solution(mesh):
    grid = Mesh(mesh.devices.reshape(8, 4, 2, 4, 2), ("z", "yh", "core", "x", "yl"))
    ex, te = ("z", "yh", "core"), ("x", "yl")
    return jax.shard_map(
        shards,
        mesh=grid,
        in_specs=(P(ex, te), P(ex, None), P(ex, None)) + (P(ex + te, None),) * 5,
        out_specs=P(ex, te),
        check_vma=False,
    )
```

```python
import jax
import jax.numpy as jnp
from jax import lax
from jax.experimental import pallas as pl
from jax.experimental.pallas import tpu as pltpu
from jax.sharding import Mesh, PartitionSpec as P

CAP = 10
HALF = CAP // 2
BLK = 40
EXP = 32
TEN = 8
BIG = 62 * 10**6
MID = 50 * 10**6
SMALL = 16 * 10**6
TOK = 128
FEAT = 448
FULL = 384
FF = 152
PAIR = 2 * FEAT
ROWS = EXP * CAP
HROWS = ROWS // 2
PIECE = 7 * HROWS
GRP = EXP // 2
FPAD = 160
D = 3584

BF = jnp.bfloat16
F32 = jnp.float32
VM = pl.BlockSpec(memory_space=pltpu.VMEM)
AN = pl.BlockSpec(memory_space=pl.ANY)


def nt(a, b):
    return lax.dot_general(a, b, (((1,), (1,)), ((), ())), preferred_element_type=F32)


def tn(a, b):
    return lax.dot_general(a, b, (((0,), (0,)), ((), ())), preferred_element_type=F32)


def block_ids(rows=BLK):
    p = lax.broadcasted_iota(jnp.int32, (EXP, rows, TOK), 0).reshape(EXP * rows, TOK)
    e = 4 * (p & 7) + (p >> 3)
    k = lax.broadcasted_iota(jnp.int32, (EXP, rows, TOK), 1).reshape(EXP * rows, TOK)
    return e, k


def slots_of(e, k):
    tens = jnp.where(k >= 30, 30, jnp.where(k >= 20, 20, jnp.where(k >= 10, 10, 0)))
    low = jnp.where(k < 35, e * CAP + k - tens, -1)
    high = jnp.where((k >= 30) & (k < 35), e * CAP + k - 30 + HALF, -1)
    return low, high


def pack_kernel(xt_ref, gt_ref, et_ref, out_ref, tgt_ref):
    yl = lax.axis_index("yl")
    e0 = et_ref[0:1, :]
    e1 = et_ref[1:2, :]
    xi = lax.broadcasted_iota(jnp.int32, (EXP, TOK), 0)
    named = ((xi == e0) | (xi == e1)).astype(F32).astype(BF)
    earlier = (
        lax.broadcasted_iota(jnp.int32, (TOK, TOK), 0) < lax.broadcasted_iota(jnp.int32, (TOK, TOK), 1)
    ).astype(F32).astype(BF)
    before = jnp.dot(named, earlier, preferred_element_type=F32)
    s0 = jnp.sum(jnp.where(xi == e0, before, 0.0), axis=0, keepdims=True).astype(jnp.int32)
    s1 = jnp.sum(jnp.where(xi == e1, before, 0.0), axis=0, keepdims=True).astype(jnp.int32)
    t0 = e0 * CAP + s0
    t1 = e1 * CAP + s1
    tgt_ref[0:1, :] = t0
    tgt_ref[1:2, :] = t1
    e, k = block_ids()
    low, high = slots_of(e, k)
    one = lambda hit: hit.astype(F32).astype(BF)
    m_low = jnp.concatenate([one(low == t0), one(low == t1)], axis=1)
    m_high = jnp.concatenate([one(high == t0), one(high == t1)], axis=1)

    def scaled(rows):
        x = rows.astype(F32)
        return jnp.concatenate([(x * gt_ref[0:1, :]).astype(BF), (x * gt_ref[1:2, :]).astype(BF)], axis=1)

    full = scaled(xt_ref[pl.ds(pl.multiple_of(64 * yl, 64), FULL), :])
    half = scaled(xt_ref[pl.ds(pl.multiple_of(FULL * (1 - yl), 64), 64), :])
    none = jnp.zeros_like(half)
    wide = nt(m_low, full)
    pair = nt(m_low, jnp.concatenate([half, none], axis=0)) + nt(m_high, jnp.concatenate([none, half], axis=0))
    picked = jnp.where(
        k < 10, wide[:, 0:128], jnp.where(k < 20, wide[:, 128:256], jnp.where(k < 30, wide[:, 256:384], pair))
    )
    out_ref[...] = picked.astype(BF)


def sort_kernel(in_ref, out_ref):
    n_in, rows = GRP * BLK, GRP * HALF
    q = lax.broadcasted_iota(jnp.int32, (rows, n_in), 0)
    col = lax.broadcasted_iota(jnp.int32, (rows, n_in), 1)
    gap = col - 35 * ((q * 205) >> 10) - q
    moves = jnp.concatenate([(gap == HALF * b).astype(F32).astype(BF) for b in range(7)], axis=0)
    both = jnp.concatenate([in_ref[0:n_in, :], in_ref[n_in : 2 * n_in, :]], axis=1)
    res = jnp.dot(moves, both, preferred_element_type=F32).astype(BF)
    for b in range(7):
        for g in range(2):
            at = b * HROWS + g * rows
            out_ref[at : at + rows, :] = res[b * rows : (b + 1) * rows, g * 128 : (g + 1) * 128]


def stack_kernel(wd0, wd1, wg0, wg1, wu0, wu1, sg0, sg1, su0, su1, w_ref, sg_ref, su_ref, f_ref):
    step = pl.program_id(0)
    def stack(ref, first, blocks):
        for i, block in enumerate(blocks):
            at = first + i * FPAD
            ref[at + FPAD - 16 : at + FPAD, :] = jnp.zeros((16, ref.shape[1]), BF)
            ref[at : at + FF, :] = block[...]

    stack(w_ref, 0, (wd0, wd1, wg0, wg1, wu0, wu1))

    @pl.when(step == 0)
    def _():
        stack(sg_ref, 0, (sg0, sg1))
        stack(su_ref, 0, (su0, su1))
        core = lax.axis_index("core")
        r = lax.broadcasted_iota(jnp.int32, (ROWS, 2 * ROWS), 0)
        col = lax.broadcasted_iota(jnp.int32, (ROWS, 2 * ROWS), 1)
        h = (r >= HROWS).astype(jnp.int32)
        q = r - HROWS * h
        p = (q * 205) >> 10
        source = 4 * (p & 7) + (p >> 3)
        pick = (col == 2 * CAP * source + (q - HALF * p) + HALF * h + CAP * core).astype(F32).astype(BF)
        g = nt(pick, sg_ref[...])
        u = nt(pick, su_ref[...])
        sig = 1.0 / (1.0 + jnp.exp(-g))
        for i, factor in enumerate((u * sig * (1.0 + g * (1.0 - sig)), g * sig)):
            high = factor.astype(BF)
            f_ref[2 * i] = high
            f_ref[2 * i + 1] = (factor - high.astype(F32)).astype(BF)

    w_ref[6 * FPAD :, 0:FULL] = jnp.concatenate([f_ref[step], jnp.zeros((ROWS, FULL - 2 * FPAD), BF)], axis=1)


def main_kernel(in_ref, w_hbm, out_ref, r_ref, w_ref, f_ref, sems):
    down, rest = 2 * FPAD, 4 * FPAD
    pairs = [(w_hbm.at[pl.ds(0, down), :], w_ref.at[pl.ds(0, down), :])]
    for i in range(4):
        pairs.append((w_hbm.at[pl.ds(down + rest, ROWS), pl.ds(i * PAIR, FULL)], f_ref.at[i]))
    for i in range(4):
        at = (pl.ds(down, rest), pl.ds(i * PAIR, PAIR))
        pairs.append((w_hbm.at[at], w_ref.at[at]))
    copies = [pltpu.make_async_copy(src, dst, sems.at[i]) for i, (src, dst) in enumerate(pairs)]
    for copy in copies:
        copy.start()
    for i in range(4):
        base, even, odd = i * PAIR, i * PIECE, (4 + i) * PIECE
        for j in range(3):
            r_ref[:, base + 128 * j : base + 128 * (j + 1)] = in_ref[even + j * ROWS : even + (j + 1) * ROWS, :]
            at = base + 512 + 128 * j
            r_ref[:, at : at + 128] = in_ref[odd + j * ROWS : odd + (j + 1) * ROWS, :]
        eh = in_ref[even + 3 * ROWS : even + PIECE, :]
        oh = in_ref[odd + 3 * ROWS : odd + PIECE, :]
        r_ref[0:HROWS, base + FULL : base + 512] = jnp.concatenate([eh[:, :64], oh[:, :64]], axis=1)
        r_ref[HROWS:ROWS, base + FULL : base + 512] = jnp.concatenate([eh[:, 64:], oh[:, 64:]], axis=1)
    copies[0].wait()
    hidden = nt(r_ref[...], w_ref[0:down, :])
    for copy in copies[1:5]:
        copy.wait()
    part = lambda i: f_ref[i, :, 0:down].astype(F32)
    grads = jnp.concatenate([hidden * (part(0) + part(1)), hidden * (part(2) + part(3))], axis=1).astype(BF)
    for i in range(4):
        base, even, odd = i * PAIR, 2 * i * PIECE, (2 * i + 1) * PIECE
        copies[5 + i].wait()
        acc = jnp.dot(grads, w_ref[down:, base : base + PAIR], preferred_element_type=F32).astype(BF)
        for j in range(3):
            out_ref[even + j * ROWS : even + (j + 1) * ROWS, :] = acc[:, 128 * j : 128 * (j + 1)]
            out_ref[odd + j * ROWS : odd + (j + 1) * ROWS, :] = acc[:, 512 + 128 * j : 512 + 128 * (j + 1)]
        lo = acc[0:HROWS, FULL:512]
        hi = acc[HROWS:ROWS, FULL:512]
        out_ref[even + 3 * ROWS : even + PIECE, :] = jnp.concatenate([lo[:, :64], hi[:, :64]], axis=1)
        out_ref[odd + 3 * ROWS : odd + PIECE, :] = jnp.concatenate([lo[:, 64:], hi[:, 64:]], axis=1)


def unsort_kernel(in_ref, out_ref):
    rows = GRP * HALF
    n_out = GRP * BLK
    q = lax.broadcasted_iota(jnp.int32, (n_out, rows), 1)
    row = lax.broadcasted_iota(jnp.int32, (n_out, rows), 0)
    gap = row - 35 * ((q * 205) >> 10) - q
    res = [None, None]
    for b in range(7):
        move = (gap == HALF * b).astype(F32).astype(BF)
        cols = []
        for g in range(2):
            total = None
            for t in range(TEN):
                at = t * PIECE + b * HROWS + g * rows
                part = in_ref[at : at + rows, :].astype(F32)
                total = part if total is None else total + part
            cols.append(total.astype(BF))
        term = jnp.dot(move, jnp.concatenate(cols, axis=1), preferred_element_type=F32)
        for g in range(2):
            t = term[:, g * 128 : (g + 1) * 128]
            res[g] = t if res[g] is None else res[g] + t
    for g in range(2):
        out_ref[g * n_out : (g + 1) * n_out, :] = res[g].astype(BF)


def combine_kernel(in_ref, tgt_ref, out_ref):
    yl = lax.axis_index("yl")
    t0 = tgt_ref[0:1, :]
    t1 = tgt_ref[1:2, :]
    e, k = block_ids()
    low, high = slots_of(e, k)
    hit = ((low == t0) | (low == t1)).astype(F32)
    cut = lambda a, b: jnp.where((k >= a) & (k < b), hit, 0.0).astype(BF)
    hit_high = ((high == t0) | (high == t1)).astype(F32).astype(BF)
    take = jnp.concatenate([cut(0, 10), cut(10, 20), cut(20, 30), cut(30, 35), hit_high], axis=1)
    res = tn(in_ref[...], take)
    start = pl.multiple_of(64 * yl, 64)
    for j in range(3):
        out_ref[pl.ds(pl.multiple_of(start + 128 * j, 64), 128), :] = res[:, 128 * j : 128 * (j + 1)].astype(BF)
    half = res[0:64, FULL:512] + res[64:128, 512:640]
    out_ref[pl.ds(pl.multiple_of(FULL * (1 - yl), 64), 64), :] = half.astype(BF)


def call(kernel, outs, specs, flops, moved, scratch=(), limit=SMALL, grid=(), out_specs=VM):
    if isinstance(outs, list) and not isinstance(out_specs, list):
        out_specs = [out_specs] * len(outs)
    return pl.pallas_call(
        kernel,
        out_shape=outs,
        grid=grid,
        in_specs=specs,
        out_specs=out_specs,
        scratch_shapes=list(scratch),
        cost_estimate=pl.CostEstimate(flops=flops, bytes_accessed=moved, transcendentals=0),
        compiler_params=pltpu.CompilerParams(vmem_limit_bytes=limit),
    )


def sds(shape, dtype=BF):
    return jax.ShapeDtypeStruct(shape, dtype)


def swap_core(a):
    return lax.ppermute(a, "core", [(0, 1), (1, 0)])


def exchange(a, axes, n):
    blocks = a.reshape(n, a.shape[0] // n, a.shape[1])
    return lax.all_to_all(blocks, axes, split_axis=0, concat_axis=0, tiled=True).reshape(a.shape)


def shards(out_grad, gate_probs, expert_ids, saved_gate, saved_up, w_gate, w_up, w_down):
    packed, target = call(
        pack_kernel,
        [sds((EXP * BLK, 128)), sds((2, TOK), jnp.int32)],
        [VM, VM, VM],
        10**9,
        10**6,
        limit=BIG,
    )(out_grad.T, gate_probs.T, expert_ids.T)
    got = exchange(packed, ("yh", "z"), EXP)
    mine = call(sort_kernel, sds((PIECE, 128)), [VM], 10**9, 10**6)(got)
    spread = jnp.broadcast_to(mine[None], (TEN, PIECE, 128)).reshape(TEN * PIECE, 128)
    pieces = exchange(spread, ("yl", "x"), TEN)

    operands = []
    for a in (w_down, w_gate, w_up, saved_gate, saved_up):
        operands += [a, swap_core(a)]
    block = pl.BlockSpec((FF, PAIR), lambda i: (0, i))
    saved = pl.BlockSpec((FF, 2 * ROWS), lambda i: (0, 0))
    weights = call(
        stack_kernel,
        sds((6 * FPAD + ROWS, D)),
        [block] * 6 + [saved] * 4,
        5 * 10**8,
        16 * 10**6,
        scratch=[pltpu.VMEM((2 * FPAD, 2 * ROWS), BF)] * 2 + [pltpu.VMEM((4, ROWS, 2 * FPAD), BF)],
        limit=BIG,
        grid=(4,),
        out_specs=pl.BlockSpec((6 * FPAD + ROWS, PAIR), lambda i: (0, i)),
    )(*operands)
    parts = call(
        main_kernel,
        sds((TEN * PIECE, 128)),
        [VM, AN],
        23 * 10**8,
        12 * 10**6,
        scratch=[
            pltpu.VMEM((ROWS, D), BF),
            pltpu.VMEM((6 * FPAD, D), BF),
            pltpu.VMEM((4, ROWS, FULL), BF),
            pltpu.SemaphoreType.DMA((9,)),
        ],
        limit=MID,
    )(pieces, weights)
    home = exchange(parts, ("x", "yl"), TEN)
    summed = call(unsort_kernel, sds((EXP * BLK, 128)), [VM], 10**9, 3 * 10**6)(home)
    back = exchange(summed, ("yh", "z"), EXP)
    out_t = call(combine_kernel, sds((FEAT, TOK)), [VM, VM], 10**9, 10**6)(back, target)
    return out_t.T


def solution(mesh):
    grid = Mesh(mesh.devices.reshape(8, 4, 2, 4, 2), ("z", "yh", "core", "x", "yl"))
    ex, te = ("z", "yh", "core"), ("x", "yl")
    return jax.shard_map(
        shards,
        mesh=grid,
        in_specs=(P(ex, te), P(ex, None), P(ex, None)) + (P(ex + te, None),) * 5,
        out_specs=P(ex, te),
        check_vma=False,
    )
```
